256 devices in a mesh: species: 8 (over z), wave: 32 (over y, x, core).
Axes of the slice: x: 4, y: 4, z: 8, core: 2. Of those that a mesh axis runs over, the one named last changes fastest.
Arguments:
- dest_tiles: int32 [8, 1024, 1], P('species', 'wave'), may hold values from 0 to 31; in each aligned block of 32 rows (0 to 31, 32 to 63, ..., all dimensions but the last counted through in order) at most 2 rows name the same one
- line_counts: int32 [8, 1024], P('species', 'wave'), may hold values from 32 to 128
- wing_widths: int32 [8, 1024], P('species', 'wave'), may hold values from 16 to 64
- species_ids: int32 [8, 131072], P('species', 'wave'), may hold values from 0 to 3
- offsets: float32 [8, 131072], P('species', 'wave'), may hold values from 0 to 256
- strengths: float32 [8, 131072], P('species', 'wave'), may hold values from 0.01 to 0.2
- doppler: float32 [8, 131072], P('species', 'wave'), may hold values from 0.5 to 6
- lorentz: float32 [8, 131072], P('species', 'wave'), may hold values from 0.1 to 4
- energy: float32 [8, 131072], P('species', 'wave'), may hold values from 0.05 to 3
- temp_scale: float32 [16], replicated, may hold values from 0.5 to 2
- press_scale: float32 [16], replicated, may hold values from 0.2 to 4
- inverse_temp: float32 [16], replicated, may hold values from 0.2 to 1.5
- abundances: float32 [4, 8, 4, 16], P(None, 'species'), may hold values from 0.05 to 1
Outputs:
- opacity: float32 [4, 16, 8192], P(None, 'species', 'wave')
The draws below stay inside these ranges and needn't reach their ends.
Inputs may be any that keep to these rules, and one draw needn't show every extreme that they name: `dest_tiles`: within one device's 32 blocks no tile is named more than 2 times.
All inputs are finite; a program needn't handle non-finite values.
Results may differ from the reference program's by a relative error of at most 0.0004.
Values sent between devices are 32-bit elements; how exact they have to be, the bound alone decides.
No kernel may reach another device: no remote copies, remote signals or barrier semaphores. Data moves between devices by JAX's collectives and lax.ppermute only.
A program may use at most 64 MiB of HBM per device.

```python
import math
import jax
import jax.numpy as jnp
import numpy as np
from jax import lax

WAVE_DEV = 256
TP = 16
MIXES = 4
SUB = 4
HALO = 64
BLOCKS_DEV = 32
MOST = 2
GROUPS = 8
LINES = 131072
BLOCKS = 1024
NWAVE = 8192
N_SPECIES = 8
N_WAVE = 32


def place_ends(values, stream_key, low, top_value):
    longest = values.shape.index(max(values.shape))
    spots = []
    for shift in (0, 1):
        where = [jax.random.randint(jax.random.fold_in(stream_key, axis), (), 0, length) for axis, length in enumerate(values.shape)]
        where[longest] = (where[longest] + shift) % values.shape[longest]
        spots.append(tuple(where))
    return values.at[spots[0]].set(low).at[spots[1]].set(top_value)


def shard_levels(rng, shape, split, smallest, high):
    factor_of = 1.0
    for axis_at, parts in split:
        heights = jax.random.uniform(jax.random.fold_in(jax.random.fold_in(rng, 6), axis_at), (parts,), jnp.float32, smallest / len(split), high / len(split))
        factor_of = factor_of * jnp.repeat(jnp.exp(heights), shape[axis_at] // parts).reshape((-1,) + (1,) * (len(shape) - 1 - axis_at))
    return factor_of


def assign_block(own_key, own, number, rows, amount, top, bound, skew):
    sequence = jax.random.permutation(own_key, amount)
    packed, ordinary = portions_of(amount, rows * top, bound, skew, True), portions_of(amount, rows * top, bound, skew, False)
    places = jnp.arange(amount)

    def named(sizes, turn):
        used = int((sizes > 0).sum())
        fixed = max(1, used // 4)
        moved = fixed + (places - fixed + turn * (used - fixed)) % max(1, amount - fixed)
        return jnp.zeros((amount,), jnp.int32).at[sequence[jnp.where(places < fixed, places, moved)]].set(jnp.asarray(sizes, jnp.int32))

    sizes = jnp.where(number % 4 == 0, named(packed, number // 4), named(ordinary, number - number // 4 - 1))
    mixed = jax.random.permutation(jax.random.fold_in(own, 3), amount)
    giver, sink = mixed[0:amount // 2 * 2:2], mixed[1:amount // 2 * 2:2]
    margin = jnp.minimum(sizes[giver] - 1, bound - sizes[sink]) // 2
    margin = jnp.where((giver == sequence[0]) | (sink == sequence[0]) | (sizes[sink] == 0), 0, jnp.maximum(margin, 0))
    moved = jax.random.randint(jax.random.fold_in(own, 4), (amount // 2,), 0, 1 << 20) % (margin + 1)
    sizes = sizes.at[giver].add(-moved).at[sink].add(moved)
    items = jnp.searchsorted(jnp.cumsum(sizes), jnp.arange(rows * top), side="right").astype(jnp.int32)
    table = items.reshape(top, rows).T
    table = table[jax.random.permutation(jax.random.fold_in(own, 1), rows)]
    turn = jax.random.randint(jax.random.fold_in(own, 2), (rows, 1), 0, top)
    return jnp.take_along_axis(table, (jnp.arange(top)[None, :] + turn) % top, axis=1)


def portions_of(amount, total, limit, skew, full):
    weights = [(1 << 20) // math.isqrt(standing ** skew) + 1 for standing in range(1, amount + 1)]
    largest = limit if full else min(limit, max(-(-total // amount), total * weights[0] // sum(weights)))
    least = 1 if total - largest >= amount - 1 else 0
    holding, spare = [largest] + [least] * (amount - 1), total - largest - least * (amount - 1)
    while spare > 0:
        free = [i for i in range(1, amount) if holding[i] < largest] or [i for i in range(1, amount) if holding[i] < limit]
        whole, left = sum([weights[i] for i in free]), spare
        for i in free:
            extra = min(limit - holding[i], max(1, left * weights[i] // whole), spare)
            holding[i] = holding[i] + extra
            spare = spare - extra
    return np.array(holding)


def setup_inputs(seed: int = 0) -> dict:
    key_of = jax.random.split(jax.random.key(seed), 14)
    dest_tiles_keys = jax.random.split(jax.random.fold_in(key_of[0], 1), GROUPS * BLOCKS // BLOCKS_DEV)
    dest_tiles_turns = jax.random.permutation(jax.random.fold_in(key_of[0], 3), GROUPS * BLOCKS // BLOCKS_DEV)
    dest_tiles = jax.vmap(lambda own, number: assign_block(jax.random.fold_in(key_of[0], 2), own, number, BLOCKS_DEV, N_WAVE, 1, MOST, 2))(dest_tiles_keys, dest_tiles_turns).reshape((GROUPS, BLOCKS, 1))
    line_counts = place_ends(jax.random.randint(key_of[1], (GROUPS, BLOCKS), 32, 129), jax.random.fold_in(key_of[1], 1), 32, 128).astype(jnp.int32)
    wing_widths = place_ends(jax.random.randint(key_of[2], (GROUPS, BLOCKS), HALO // 4, HALO + 1), jax.random.fold_in(key_of[2], 1), HALO // 4, HALO).astype(jnp.int32)
    species_ids = place_ends(jax.random.randint(key_of[3], (GROUPS, LINES), 0, SUB), jax.random.fold_in(key_of[3], 1), 0, SUB - 1).astype(jnp.int32)
    offsets = jnp.clip(256.0 * jax.random.uniform(key_of[4], (GROUPS, LINES), jnp.float32) ** shard_levels(key_of[4], (GROUPS, LINES), ((0, 8), (1, 32)), -0.2, 0.2), 0.0, 256.0)
    strengths = jnp.clip(jnp.exp(math.log(0.2) - 2.9957323 * jax.random.uniform(key_of[5], (GROUPS, LINES), jnp.float32) ** shard_levels(key_of[5], (GROUPS, LINES), ((0, 8), (1, 32)), -0.2, 0.2)), 0.01, 0.2)
    doppler = jnp.clip(jnp.exp(math.log(6.0) - 2.4849066 * jax.random.uniform(key_of[6], (GROUPS, LINES), jnp.float32) ** shard_levels(key_of[6], (GROUPS, LINES), ((0, 8), (1, 32)), -0.2, 0.2)), 0.5, 6.0)
    lorentz = jnp.clip(jnp.exp(math.log(4.0) - 3.6888794 * jax.random.uniform(key_of[7], (GROUPS, LINES), jnp.float32) ** shard_levels(key_of[7], (GROUPS, LINES), ((0, 8), (1, 32)), -0.2, 0.2)), 0.1, 4.0)
    energy = jnp.clip(jnp.exp(math.log(3.0) - 4.0943445 * jax.random.uniform(key_of[8], (GROUPS, LINES), jnp.float32) ** shard_levels(key_of[8], (GROUPS, LINES), ((0, 8), (1, 32)), -0.2, 0.2)), 0.05, 3.0)
    temp_scale = jnp.clip(jnp.exp(jax.random.uniform(key_of[9], (TP,), jnp.float32, math.log(0.5), math.log(2.0))), 0.5, 2.0)
    press_scale = jnp.clip(jnp.exp(jax.random.uniform(key_of[10], (TP,), jnp.float32, math.log(0.2), math.log(4.0))), 0.2, 4.0)
    inverse_temp = jnp.clip(jax.random.uniform(key_of[11], (TP,), jnp.float32, 0.2, 1.5), 0.2, 1.5)
    abundances = jnp.clip(jnp.exp(math.log(1.0) - 2.9957323 * jax.random.uniform(key_of[12], (MIXES, GROUPS, SUB, TP), jnp.float32) ** shard_levels(key_of[12], (MIXES, GROUPS, SUB, TP), ((1, 8),), -0.2, 0.2)), 0.05, 1.0)
    return {"dest_tiles": dest_tiles, "line_counts": line_counts, "wing_widths": wing_widths, "species_ids": species_ids, "offsets": offsets, "strengths": strengths, "doppler": doppler, "lorentz": lorentz, "energy": energy, "temp_scale": temp_scale, "press_scale": press_scale, "inverse_temp": inverse_temp, "abundances": abundances}


def profile(center, doppler_row, lorentz_row, wing_reach, temp_scale, press_scale, extent):
    doppler_width = temp_scale[:, None] * doppler_row[None, :]
    pressure_width = press_scale[:, None] * lorentz_row[None, :]
    gauss_full = 2.35482 * doppler_width
    lorentz_full = 2.0 * pressure_width
    voigt_width = (gauss_full ** 5 + 2.69269 * gauss_full ** 4 * lorentz_full
                   + 2.42843 * gauss_full ** 3 * lorentz_full ** 2
                   + 4.47163 * gauss_full ** 2 * lorentz_full ** 3
                   + 0.07842 * gauss_full * lorentz_full ** 4 + lorentz_full ** 5) ** 0.2
    lorentz_ratio = lorentz_full / voigt_width
    mixing = 1.36603 * lorentz_ratio - 0.47719 * lorentz_ratio * lorentz_ratio + 0.11116 * lorentz_ratio * lorentz_ratio * lorentz_ratio
    points = jnp.arange(extent).astype(jnp.float32) - HALO
    offset = points[None, None, :] - center[None, :, None]
    square = offset * offset
    voigt_col = voigt_width[:, :, None]
    gauss_shape = (0.9394373 / voigt_col) * jnp.exp(-2.7725887 * square / (voigt_col * voigt_col))
    lorentz_shape = (0.15915494 * voigt_col) / (square + 0.25 * voigt_col * voigt_col)
    mix_col = mixing[:, :, None]
    profile_values = mix_col * lorentz_shape + (1.0 - mix_col) * gauss_shape
    return jnp.where(jnp.abs(offset) <= wing_reach[None, :, None], profile_values, 0.0)


def mix_weights(abund_group, per_species, energy_row, inverse_temp):
    boltzmann = jnp.exp(-inverse_temp[:, None] * energy_row[None, :])
    summed = jnp.sum(abund_group[:, :, :, None] * per_species[None, :, None, :], axis=1)
    return summed * boltzmann[None]


def regroup(array):
    return array.reshape((array.shape[0] // 8, 8) + array.shape[1:])


def reference(dest_tiles, line_counts, wing_widths, species_ids, offsets, strengths, doppler, lorentz, energy, temp_scale, press_scale, inverse_temp, abundances):
    nblocks = BLOCKS_DEV * N_WAVE
    extent = WAVE_DEV + 2 * HALO
    lanes = jnp.arange(128)
    kinds = jnp.arange(SUB)
    canvas = jnp.zeros((MIXES, TP, NWAVE + 2 * HALO), jnp.float32)
    for group in range(N_SPECIES):
        live = lanes[None, :] < line_counts[group][:, None]
        kind_rows = species_ids[group].reshape(nblocks, 128)
        base = jnp.where(live, strengths[group].reshape(nblocks, 128), 0.0)
        per_species = jnp.where(kind_rows[:, None, :] == kinds[None, :, None], base[:, None, :], 0.0)
        fields = (dest_tiles[group, :, 0], wing_widths[group].astype(jnp.float32),
                  offsets[group].reshape(nblocks, 128), doppler[group].reshape(nblocks, 128),
                  lorentz[group].reshape(nblocks, 128), energy[group].reshape(nblocks, 128), per_species)
        batched = jax.tree.map(regroup, fields)
        abund_group = abundances[:, group]

        def advance(canvas, item):
            tiles, reach, center, dop_rows, lor_rows, energy_rows, strength_rows = item
            for slot in range(8):
                reach_row = jnp.broadcast_to(reach[slot], (128,))
                values = profile(center[slot], dop_rows[slot], lor_rows[slot], reach_row, temp_scale, press_scale, extent).astype(jnp.bfloat16)
                weights = mix_weights(abund_group, strength_rows[slot], energy_rows[slot], inverse_temp).astype(jnp.bfloat16)
                part = jnp.einsum("mtl,tln->mtn", weights.astype(jnp.float32), values.astype(jnp.float32), precision=lax.Precision.HIGHEST)
                start = (tiles[slot] * WAVE_DEV).astype(jnp.int32)
                zero = jnp.zeros((), jnp.int32)
                window = lax.dynamic_slice(canvas, (zero, zero, start), (MIXES, TP, extent))
                canvas = lax.dynamic_update_slice(canvas, window + part, (zero, zero, start))
            return canvas, None

        canvas = lax.scan(advance, canvas, batched)[0]
    return canvas[:, :, HALO:HALO + NWAVE]
```

```python
import jax
import jax.numpy as jnp
from jax import lax
from jax.experimental import pallas as pl
from jax.experimental.pallas import tpu as pltpu
from jax.sharding import PartitionSpec as P

TILE = 256
TP = 16
MIXES = 4
SUB = 4
HALO = 64
LANES = 128
FIELDS = 8
BUCKET = 16
NBUCKET = TILE // BUCKET + 1
ROWS = 2 * HALO + BUCKET
COLS = 80
STEP = 8
CLASSES = HALO // STEP
UNROLL = 2

VMEM = pl.BlockSpec(memory_space=pltpu.VMEM)
SMEM = pl.BlockSpec(memory_space=pltpu.SMEM)


def pack_kernel(nblocks, dest, counts, reach, off, dop, lor, ene, stre, spec, out, used):
    ntiles = used.shape[0]
    row = lax.broadcasted_iota(jnp.int32, (FIELDS, LANES), 0)
    blank = jnp.where((row == 1) | (row == 2), 1.0, 0.0)

    def clear(tile, _):
        used[tile] = 0
        out[2 * tile] = blank
        out[2 * tile + 1] = blank
        return 0

    lax.fori_loop(0, ntiles, clear, 0, unroll=4)
    lane = lax.broadcasted_iota(jnp.int32, (1, LANES), 1)

    def place(block, _):
        tile = dest[block]
        rank = used[tile]
        used[tile] = rank + 1
        slot = 2 * tile + rank
        at = pl.ds(block, 1)
        out[slot, 0:1, :] = off[at, :]
        out[slot, 1:2, :] = dop[at, :]
        out[slot, 2:3, :] = lor[at, :]
        out[slot, 3:4, :] = ene[at, :]
        out[slot, 4:5, :] = jnp.where(lane < counts[block], stre[at, :], 0.0)
        out[slot, 5:6, :] = spec[at, :].astype(jnp.float32)
        out[slot, 6:7, :] = jnp.full((1, LANES), reach[block].astype(jnp.float32))
        return 0

    lax.fori_loop(0, nblocks, place, 0, unroll=4)


def opacity_kernel(nslots, reach, recs, abund, temps, acc, order, first, prm, wts, hot, sq):
    def count(i, _):
        c = lax.shift_right_logical(reach[i] + (STEP - 1), 3)
        first[c] = first[c] + 1
        return 0

    def klass(i):
        return lax.shift_right_logical(reach[i] + (STEP - 1), 3)

    for c in range(CLASSES + 1):
        first[c] = 0
    lax.fori_loop(0, nslots, count, 0, unroll=8)
    total = jnp.int32(0)
    starts = {}
    for c in range(CLASSES, -1, -1):
        starts[c] = total
        held = first[c]
        first[c] = total
        total = total + held

    def place(i, _):
        c = klass(i)
        at = first[c]
        order[at] = i
        first[c] = at + 1
        return 0

    lax.fori_loop(0, nslots, place, 0, unroll=8)

    def wipe(t, _):
        acc[t] = jnp.zeros(acc.shape[1:], jnp.float32)
        return 0

    lax.fori_loop(0, TP, wipe, 0)

    tscale, pscale, invt = temps[:, 0:1], temps[:, 1:2], temps[:, 2:3]
    bucket_row = lax.shift_right_logical(lax.broadcasted_iota(jnp.int32, (COLS, 2 * LANES), 0), 2)
    bucket_row = bucket_row.astype(jnp.float32)

    def pair(p, far):
        n = 2 * far + BUCKET
        rec = jnp.concatenate([recs[order[2 * p]], recs[order[2 * p + 1]]], axis=1)
        center, dop, lor, energy = rec[0:1], rec[1:2], rec[2:3], rec[3:4]
        strength, kind, limit = rec[4:5], rec[5:6], rec[6:7]
        gauss = 2.35482 * (tscale * dop)
        lorz = 2.0 * (pscale * lor)
        g2, l2 = gauss * gauss, lorz * lorz
        g4, l4 = g2 * g2, l2 * l2
        fifth = (
            g4 * gauss
            + 2.69269 * g4 * lorz
            + 2.42843 * (g2 * gauss) * l2
            + 4.47163 * g2 * (l2 * lorz)
            + 0.07842 * gauss * l4
            + l4 * lorz
        )
        width = jnp.exp(0.2 * jnp.log(fifth))
        inv = 1.0 / width
        q = lorz * inv
        mixing = q * (1.36603 + q * (-0.47719 + q * 0.11116))
        prm[0] = mixing * (0.15915494 * width)
        prm[1] = 0.25 * (width * width)
        prm[2] = (1.0 - mixing) * (0.9394373 * inv)
        prm[3] = (-2.7725887 * 1.4426950408889634) * (inv * inv)
        boltz = jnp.exp(-(invt * energy))
        prm[4] = boltz
        bucket = jnp.floor(center * (1.0 / BUCKET))
        frac = center - BUCKET * bucket
        hot[...] = jnp.where(bucket_row == bucket, 1.0, 0.0).astype(jnp.bfloat16)
        point = lax.broadcasted_iota(jnp.int32, (n, 2 * LANES), 0).astype(jnp.float32) - float(far)
        x = point - frac
        sq[0:n] = jnp.where(jnp.abs(x) <= limit, x * x, jnp.inf)

        def at_point(t, _):
            picked = jnp.zeros((8, 2 * LANES), jnp.float32)
            for s in range(SUB):
                ab = abund[t, s]
                picked = jnp.where(kind == float(s), jnp.concatenate([ab, ab], axis=1), picked)
            w8 = picked * strength * prm[4, pl.ds(t, 1), :]
            w16 = jnp.concatenate([w8, w8], axis=0).astype(jnp.bfloat16)
            wide = hot[...] * jnp.concatenate([w16] * (COLS // 16), axis=0)
            a = prm[0, pl.ds(t, 1), :]
            b = prm[1, pl.ds(t, 1), :]
            g = prm[2, pl.ds(t, 1), :]
            h = prm[3, pl.ds(t, 1), :]
            s2 = sq[0:n]
            shape = a * pl.reciprocal(s2 + b, approx=True) + g * jnp.exp2(s2 * h)
            part = lax.dot_general(
                shape.astype(jnp.bfloat16),
                wide,
                (((1,), (1,)), ((), ())),
                preferred_element_type=jnp.float32,
            )
            low = HALO - far
            acc[t, low : low + n, 0:COLS] = acc[t, low : low + n, 0:COLS] + part
            return 0

        lax.fori_loop(0, TP, at_point, 0, unroll=UNROLL)

    for c in range(CLASSES, 0, -1):
        begin = lax.shift_right_logical(starts[c] + 1, 1)
        end = lax.shift_right_logical(starts[c - 1] + 1, 1)

        def body(p, _, far=STEP * c):
            pair(p, far)
            return 0

        lax.fori_loop(begin, end, body, 0)


def fold_kernel(acc, out):
    for t in range(TP):
        total = acc[t, 0:BUCKET, :]
        for i in range(1, ROWS // BUCKET):
            total = total + pltpu.roll(acc[t, BUCKET * i : BUCKET * (i + 1), :], MIXES * i, 1)
        out[t] = total


def opacity(reach, recs, abund, temps):
    nslots = recs.shape[0]

    def kernel(reach, recs, abund, temps, out, acc, *scratch):
        opacity_kernel(nslots, reach, recs, abund, temps, acc, *scratch)
        fold_kernel(acc, out)

    return pl.pallas_call(
        kernel,
        out_shape=jax.ShapeDtypeStruct((TP, BUCKET, LANES), jnp.float32),
        in_specs=[SMEM, VMEM, VMEM, VMEM],
        out_specs=VMEM,
        scratch_shapes=[
            pltpu.VMEM((TP, ROWS, LANES), jnp.float32),
            pltpu.SMEM((nslots,), jnp.int32),
            pltpu.SMEM((CLASSES + 1,), jnp.int32),
            pltpu.VMEM((5, TP, 2 * LANES), jnp.float32),
            pltpu.VMEM((8, LANES), jnp.float32),
            pltpu.VMEM((COLS, 2 * LANES), jnp.bfloat16),
            pltpu.VMEM((ROWS, 2 * LANES), jnp.float32),
        ],
        compiler_params=pltpu.CompilerParams(vmem_limit_bytes=24 * 2**20),
        name="opacity",
    )(reach, recs, abund, temps)


def per_device(
    dest_tiles,
    line_counts,
    wing_widths,
    species_ids,
    offsets,
    strengths,
    doppler,
    lorentz,
    energy,
    temp_scale,
    press_scale,
    inverse_temp,
    abundances,
):
    ntiles = lax.axis_size("wave")
    nblocks = dest_tiles.shape[1]

    def rows(array):
        return array.reshape(nblocks, LANES)

    packed = pl.pallas_call(
        lambda *refs: pack_kernel(nblocks, *refs),
        out_shape=jax.ShapeDtypeStruct((2 * ntiles, FIELDS, LANES), jnp.float32),
        in_specs=[SMEM] * 3 + [VMEM] * 6,
        out_specs=VMEM,
        scratch_shapes=[pltpu.SMEM((ntiles,), jnp.int32)],
        name="pack",
    )(
        dest_tiles.reshape(nblocks),
        line_counts.reshape(nblocks),
        wing_widths.reshape(nblocks),
        rows(offsets),
        rows(doppler),
        rows(lorentz),
        rows(energy),
        rows(strengths),
        rows(species_ids),
    )
    recs = lax.all_to_all(packed, "wave", split_axis=0, concat_axis=0, tiled=True)
    reach = recs[:, 6, 0].astype(jnp.int32)
    abund = jnp.transpose(abundances[:, 0], (2, 1, 0))
    abund = jnp.tile(abund, (1, 1, 2))[..., None] + jnp.zeros((LANES,), jnp.float32)
    temps = jnp.stack([temp_scale, press_scale, inverse_temp], axis=1)
    summed = opacity(reach, recs, abund, temps)
    shares = lax.all_to_all(summed, "species", split_axis=0, concat_axis=0, tiled=True)
    mine = jnp.sum(shares.reshape(-1, TP // lax.axis_size("species"), BUCKET, LANES), axis=0)

    below, above = mine[:, :, : 4 * MIXES], mine[:, :, 20 * MIXES : 24 * MIXES]
    up = [(i, i + 1) for i in range(ntiles - 1)]
    down = [(i + 1, i) for i in range(ntiles - 1)]
    from_left = lax.ppermute(above, "wave", up)
    from_right = lax.ppermute(below, "wave", down)
    middle = mine[:, :, 4 * MIXES : 20 * MIXES]
    width = ((0, 0), (0, 0))
    middle = (
        middle
        + jnp.pad(from_left, width + ((0, 12 * MIXES),))
        + jnp.pad(from_right, width + ((12 * MIXES, 0),))
    )
    middle = middle.reshape(-1, BUCKET, TILE // BUCKET, MIXES)
    return jnp.transpose(middle, (3, 0, 2, 1)).reshape(MIXES, -1, TILE)


def solution(mesh):
    line = P("species", "wave")
    return jax.shard_map(
        per_device,
        mesh=mesh,
        in_specs=(P("species", "wave", None),) + (line,) * 8 + (P(), P(), P(), P(None, "species", None, None)),
        out_specs=P(None, "species", "wave"),
        check_vma=False,
    )
```

```python
import jax
import jax.numpy as jnp
from jax import lax
from jax.experimental import pallas as pl
from jax.experimental.pallas import tpu as pltpu
from jax.sharding import PartitionSpec as P

TILE = 256
TP = 16
MIXES = 4
SUB = 4
HALO = 64
LANES = 128
FIELDS = 8
BUCKET = 16
NBUCKET = TILE // BUCKET + 1
ROWS = 2 * HALO + BUCKET
COLS = 80
STEP = 8
CLASSES = HALO // STEP
UNROLL = 16
PREP = 4
POUR = 4

VMEM = pl.BlockSpec(memory_space=pltpu.VMEM)
SMEM = pl.BlockSpec(memory_space=pltpu.SMEM)


def pack_kernel(nblocks, dest, counts, reach, off, dop, lor, ene, stre, spec, out, used):
    ntiles = used.shape[0]
    empty = jnp.zeros((FIELDS, LANES), jnp.float32)

    def clear(tile, _):
        used[tile] = 0
        out[2 * tile] = empty
        out[2 * tile + 1] = empty
        return 0

    lax.fori_loop(0, ntiles, clear, 0, unroll=4)

    def place(block, _):
        tile = dest[block]
        rank = used[tile]
        used[tile] = rank + 1
        slot = 2 * tile + rank
        at = pl.ds(block, 1)
        out[slot, 0:1, :] = off[at, :]
        out[slot, 1:2, :] = dop[at, :]
        out[slot, 2:3, :] = lor[at, :]
        out[slot, 3:4, :] = ene[at, :]
        out[slot, 4:5, :] = stre[at, :]
        out[slot, 5:6, :] = spec[at, :].astype(jnp.float32)
        out[slot, 6:7, :] = jnp.full((1, LANES), reach[block].astype(jnp.float32))
        out[slot, 7:8, :] = jnp.full((1, LANES), counts[block].astype(jnp.float32))
        return 0

    lax.fori_loop(0, nblocks, place, 0, unroll=4)


def opacity_kernel(nslots, scalars, recs, abund, temps, acc, order, first, lines, live, prm, hot, sq):
    def klass(i):
        return lax.shift_right_logical(scalars[0, i] + (STEP - 1), 3)

    def count(i, _):
        c = klass(i)
        first[c] = first[c] + 1
        lines[c] = lines[c] + scalars[1, i]
        return 0

    for c in range(CLASSES + 1):
        first[c] = 0
        lines[c] = 0
    lax.fori_loop(0, nslots, count, 0, unroll=8)
    slots, total = jnp.int32(0), jnp.int32(0)
    ends = {CLASSES + 1: total}
    for c in range(CLASSES, 0, -1):
        held = first[c]
        first[c] = slots
        slots = slots + held
        total = total + lines[c]
        ends[c] = lax.shift_right_logical(total + (2 * LANES - 1), 8)
    first[0] = slots

    def place(i, _):
        c = klass(i)
        at = first[c]
        order[at] = i
        first[c] = at + 1
        return 0

    lax.fori_loop(0, nslots, place, 0, unroll=8)

    row = lax.broadcasted_iota(jnp.int32, (FIELDS, LANES), 0)
    lane = lax.broadcasted_iota(jnp.int32, (FIELDS, LANES), 1)
    blank = jnp.where((row == 1) | (row == 2), 1.0, 0.0)

    def empty(i, _):
        live[i] = blank
        return 0

    lax.fori_loop(0, live.shape[0], empty, 0, unroll=6)

    def pour(i, filled):
        for j in range(POUR):
            slot = order[POUR * i + j]
            held = scalars[1, slot]
            into = lax.shift_right_logical(filled, 7)
            turn = lax.bitwise_and(filled, LANES - 1)
            turned = pltpu.roll(recs[slot], turn, 1)
            pltpu.store(live.at[into], turned, mask=(lane >= turn) & (lane < turn + held))
            pltpu.store(live.at[into + 1], turned, mask=lane < turn + held - LANES)
            filled = filled + held
        return filled

    lax.fori_loop(0, lax.div(slots + (POUR - 1), POUR), pour, jnp.int32(0))

    def wipe(t, _):
        acc[t] = jnp.zeros(acc.shape[1:], jnp.float32)
        return 0

    lax.fori_loop(0, TP, wipe, 0)

    tscale, pscale, invt = temps[:, 0:1], temps[:, 1:2], temps[:, 2:3]
    bucket_row = lax.shift_right_logical(lax.broadcasted_iota(jnp.int32, (COLS, 2 * LANES), 0), 2)
    bucket_row = bucket_row.astype(jnp.float32)

    def prepare(p):
        rec = jnp.concatenate([live[2 * p], live[2 * p + 1]], axis=1)
        dop, lor, energy = rec[1:2], rec[2:3], rec[3:4]
        gauss = 2.35482 * (tscale * dop)
        lorz = 2.0 * (pscale * lor)
        g2, l2 = gauss * gauss, lorz * lorz
        g4, l4 = g2 * g2, l2 * l2
        fifth = (
            g4 * gauss
            + 2.69269 * g4 * lorz
            + 2.42843 * (g2 * gauss) * l2
            + 4.47163 * g2 * (l2 * lorz)
            + 0.07842 * gauss * l4
            + l4 * lorz
        )
        width = jnp.exp(0.2 * jnp.log(fifth))
        inv = 1.0 / width
        q = lorz * inv
        mixing = q * (1.36603 + q * (-0.47719 + q * 0.11116))
        prm[p, 0] = mixing * (0.15915494 * width)
        prm[p, 1] = 0.25 * (width * width)
        prm[p, 2] = (1.0 - mixing) * (0.9394373 * inv)
        prm[p, 3] = (-2.7725887 * 1.4426950408889634) * (inv * inv)
        prm[p, 4] = jnp.exp(-(invt * energy))

    def prepare_some(i, _):
        for j in range(PREP):
            prepare(PREP * i + j)
        return 0

    lax.fori_loop(0, lax.div(ends[1] + (PREP - 1), PREP), prepare_some, 0)

    def pair(p, far):
        n = 2 * far + BUCKET
        rec = jnp.concatenate([live[2 * p], live[2 * p + 1]], axis=1)
        center, strength, kind, limit = rec[0:1], rec[4:5], rec[5:6], rec[6:7]
        bucket = jnp.floor(center * (1.0 / BUCKET))
        frac = center - BUCKET * bucket
        hot[...] = jnp.where(bucket_row == bucket, 1.0, 0.0).astype(jnp.bfloat16)
        point = lax.broadcasted_iota(jnp.int32, (n, 2 * LANES), 0).astype(jnp.float32) - float(far)
        x = point - frac
        sq[0:n] = jnp.where(jnp.abs(x) <= limit, x * x, jnp.inf)

        def at_point(t, _):
            at = pl.ds(t, 1)
            picked = jnp.zeros((8, 2 * LANES), jnp.float32)
            for s in range(SUB):
                ab = abund[t, s]
                picked = jnp.where(kind == float(s), jnp.concatenate([ab, ab], axis=1), picked)
            w8 = picked * strength * prm[p, 4, at, :]
            w16 = jnp.concatenate([w8, w8], axis=0).astype(jnp.bfloat16)
            wide = hot[...] * jnp.concatenate([w16] * (COLS // 16), axis=0)
            a, b, g, h = [prm[p, j, at, :] for j in range(4)]
            s2 = sq[0:n]
            shape = a * pl.reciprocal(s2 + b, approx=True) + g * jnp.exp2(s2 * h)
            part = lax.dot_general(
                shape.astype(jnp.bfloat16),
                wide,
                (((1,), (1,)), ((), ())),
                preferred_element_type=jnp.float32,
            )
            low = HALO - far
            acc[t, low : low + n, 0:COLS] = acc[t, low : low + n, 0:COLS] + part
            return 0

        lax.fori_loop(0, TP, at_point, 0, unroll=UNROLL)

    for c in range(CLASSES, 0, -1):
        def body(p, _, far=STEP * c):
            pair(p, far)
            return 0

        lax.fori_loop(ends[c + 1], ends[c], body, 0)


def fold_kernel(acc, out):
    for t in range(TP):
        total = acc[t, 0:BUCKET, :]
        for i in range(1, ROWS // BUCKET):
            total = total + pltpu.roll(acc[t, BUCKET * i : BUCKET * (i + 1), :], MIXES * i, 1)
        out[t] = total


def opacity(scalars, recs, abund, temps):
    nslots = recs.shape[0]

    def kernel(scalars, recs, abund, temps, out, acc, *scratch):
        opacity_kernel(nslots, scalars, recs, abund, temps, acc, *scratch)
        fold_kernel(acc, out)

    return pl.pallas_call(
        kernel,
        out_shape=jax.ShapeDtypeStruct((TP, BUCKET, LANES), jnp.float32),
        in_specs=[SMEM, VMEM, VMEM, VMEM],
        out_specs=VMEM,
        scratch_shapes=[
            pltpu.VMEM((TP, ROWS, LANES), jnp.float32),
            pltpu.SMEM((nslots,), jnp.int32),
            pltpu.SMEM((CLASSES + 1,), jnp.int32),
            pltpu.SMEM((CLASSES + 1,), jnp.int32),
            pltpu.VMEM((nslots + 2, FIELDS, LANES), jnp.float32),
            pltpu.VMEM((nslots // 2, 5, TP, 2 * LANES), jnp.float32),
            pltpu.VMEM((COLS, 2 * LANES), jnp.bfloat16),
            pltpu.VMEM((ROWS, 2 * LANES), jnp.float32),
        ],
        compiler_params=pltpu.CompilerParams(vmem_limit_bytes=24 * 2**20),
        name="opacity",
    )(scalars, recs, abund, temps)


def per_device(
    dest_tiles,
    line_counts,
    wing_widths,
    species_ids,
    offsets,
    strengths,
    doppler,
    lorentz,
    energy,
    temp_scale,
    press_scale,
    inverse_temp,
    abundances,
):
    ntiles = lax.axis_size("wave")
    nblocks = dest_tiles.shape[1]

    def rows(array):
        return array.reshape(nblocks, LANES)

    packed = pl.pallas_call(
        lambda *refs: pack_kernel(nblocks, *refs),
        out_shape=jax.ShapeDtypeStruct((2 * ntiles, FIELDS, LANES), jnp.float32),
        in_specs=[SMEM] * 3 + [VMEM] * 6,
        out_specs=VMEM,
        scratch_shapes=[pltpu.SMEM((ntiles,), jnp.int32)],
        name="pack",
    )(
        dest_tiles.reshape(nblocks),
        line_counts.reshape(nblocks),
        wing_widths.reshape(nblocks),
        rows(offsets),
        rows(doppler),
        rows(lorentz),
        rows(energy),
        rows(strengths),
        rows(species_ids),
    )
    recs = lax.all_to_all(packed, "wave", split_axis=0, concat_axis=0, tiled=True)
    scalars = jnp.transpose(recs[:, 6:8, 0]).astype(jnp.int32)
    abund = jnp.transpose(abundances[:, 0], (2, 1, 0))
    abund = jnp.tile(abund, (1, 1, 2))[..., None] + jnp.zeros((LANES,), jnp.float32)
    temps = jnp.stack([temp_scale, press_scale, inverse_temp], axis=1)
    summed = opacity(scalars, recs, abund, temps)
    shares = lax.all_to_all(summed, "species", split_axis=0, concat_axis=0, tiled=True)
    mine = jnp.sum(shares.reshape(-1, TP // lax.axis_size("species"), BUCKET, LANES), axis=0)

    below, above = mine[:, :, : 4 * MIXES], mine[:, :, 20 * MIXES : 24 * MIXES]
    up = [(i, i + 1) for i in range(ntiles - 1)]
    down = [(i + 1, i) for i in range(ntiles - 1)]
    from_left = lax.ppermute(above, "wave", up)
    from_right = lax.ppermute(below, "wave", down)
    middle = mine[:, :, 4 * MIXES : 20 * MIXES]
    width = ((0, 0), (0, 0))
    middle = (
        middle
        + jnp.pad(from_left, width + ((0, 12 * MIXES),))
        + jnp.pad(from_right, width + ((12 * MIXES, 0),))
    )
    middle = middle.reshape(-1, BUCKET, TILE // BUCKET, MIXES)
    return jnp.transpose(middle, (3, 0, 2, 1)).reshape(MIXES, -1, TILE)


def solution(mesh):
    line = P("species", "wave")
    return jax.shard_map(
        per_device,
        mesh=mesh,
        in_specs=(P("species", "wave", None),) + (line,) * 8 + (P(), P(), P(), P(None, "species", None, None)),
        out_specs=P(None, "species", "wave"),
        check_vma=False,
    )
```

```python
import jax
import jax.numpy as jnp
from jax import lax
from jax.experimental import pallas as pl
from jax.experimental.pallas import tpu as pltpu
from jax.sharding import PartitionSpec as P

TILE = 256
TP = 16
MIXES = 4
SUB = 4
HALO = 64
LANES = 128
FIELDS = 8
BUCKET = 16
NBUCKET = TILE // BUCKET
ROWS = 2 * HALO + BUCKET
COLS = 2 * NBUCKET * MIXES
STEP = 8
CLASSES = HALO // STEP
UNROLL = 16
GROUP = 4
PREP = 2
POUR = 4

VMEM = pl.BlockSpec(memory_space=pltpu.VMEM)
SMEM = pl.BlockSpec(memory_space=pltpu.SMEM)


def pack_kernel(nblocks, dest, counts, reach, off, dop, lor, ene, stre, spec, out, used):
    ntiles = used.shape[0]
    empty = jnp.zeros((FIELDS, LANES), jnp.float32)

    def clear(tile, _):
        used[tile] = 0
        out[2 * tile] = empty
        out[2 * tile + 1] = empty
        return 0

    lax.fori_loop(0, ntiles, clear, 0, unroll=4)

    def place(block, _):
        tile = dest[block]
        rank = used[tile]
        used[tile] = rank + 1
        slot = 2 * tile + rank
        at = pl.ds(block, 1)
        out[slot, 0:1, :] = off[at, :]
        out[slot, 1:2, :] = dop[at, :]
        out[slot, 2:3, :] = lor[at, :]
        out[slot, 3:4, :] = ene[at, :]
        out[slot, 4:5, :] = stre[at, :]
        out[slot, 5:6, :] = spec[at, :].astype(jnp.float32)
        out[slot, 6:7, :] = jnp.full((1, LANES), reach[block].astype(jnp.float32))
        out[slot, 7:8, :] = jnp.full((1, LANES), counts[block].astype(jnp.float32))
        return 0

    lax.fori_loop(0, nblocks, place, 0, unroll=4)


def opacity_kernel(nslots, scalars, recs, abund, temps, acc, order, first, lines, live, prm, hot, sq):
    def klass(i):
        wing = scalars[0, i]
        c = jnp.minimum(lax.shift_right_logical(wing, 3) + 1, CLASSES)
        return jnp.where(wing > 0, c, 0)

    def count(i, _):
        c = klass(i)
        first[c] = first[c] + 1
        lines[c] = lines[c] + scalars[1, i]
        return 0

    for c in range(CLASSES + 1):
        first[c] = 0
        lines[c] = 0
    lax.fori_loop(0, nslots, count, 0, unroll=8)
    slots, total = jnp.int32(0), jnp.int32(0)
    ends = {CLASSES + 1: total}
    for c in range(CLASSES, 0, -1):
        held = first[c]
        first[c] = slots
        slots = slots + held
        total = total + lines[c]
        ends[c] = lax.div(total + (GROUP * LANES - 1), GROUP * LANES)
    first[0] = slots

    def place(i, _):
        c = klass(i)
        at = first[c]
        order[at] = i
        first[c] = at + 1
        return 0

    lax.fori_loop(0, nslots, place, 0, unroll=8)

    row = lax.broadcasted_iota(jnp.int32, (FIELDS, LANES), 0)
    lane = lax.broadcasted_iota(jnp.int32, (FIELDS, LANES), 1)
    blank = jnp.where((row == 1) | (row == 2), 1.0, 0.0)

    def empty(i, _):
        live[i] = blank
        return 0

    lax.fori_loop(0, live.shape[0], empty, 0, unroll=6)

    def pour(i, filled):
        for j in range(POUR):
            slot = order[POUR * i + j]
            held = scalars[1, slot]
            into = lax.shift_right_logical(filled, 7)
            turn = lax.bitwise_and(filled, LANES - 1)
            side = lax.bitwise_and(lax.shift_right_logical(slot, 1), 1)
            record = jnp.where(row == 7, side.astype(jnp.float32), recs[slot])
            turned = pltpu.roll(record, turn, 1)
            pltpu.store(live.at[into], turned, mask=(lane >= turn) & (lane < turn + held))
            pltpu.store(live.at[into + 1], turned, mask=lane < turn + held - LANES)
            filled = filled + held
        return filled

    lax.fori_loop(0, lax.div(slots + (POUR - 1), POUR), pour, jnp.int32(0))

    def wipe(t, _):
        acc[t] = jnp.zeros(acc.shape[1:], jnp.float32)
        return 0

    lax.fori_loop(0, TP, wipe, 0)

    tscale, pscale, invt = temps[:, 0:1], temps[:, 1:2], temps[:, 2:3]
    bucket_row = lax.shift_right_logical(lax.broadcasted_iota(jnp.int32, (COLS, GROUP * LANES), 0), 2)
    bucket_row = bucket_row.astype(jnp.float32)

    def prepare(p):
        rec = jnp.concatenate([live[GROUP * p + j] for j in range(GROUP)], axis=1)
        dop, lor, energy = rec[1:2], rec[2:3], rec[3:4]
        gauss = 2.35482 * (tscale * dop)
        lorz = 2.0 * (pscale * lor)
        g2, l2 = gauss * gauss, lorz * lorz
        g4, l4 = g2 * g2, l2 * l2
        fifth = (
            g4 * gauss
            + 2.69269 * g4 * lorz
            + 2.42843 * (g2 * gauss) * l2
            + 4.47163 * g2 * (l2 * lorz)
            + 0.07842 * gauss * l4
            + l4 * lorz
        )
        width = jnp.exp(0.2 * jnp.log(fifth))
        inv = 1.0 / width
        q = lorz * inv
        mixing = q * (1.36603 + q * (-0.47719 + q * 0.11116))
        prm[p, 0] = mixing * (0.15915494 * width)
        prm[p, 1] = 0.25 * (width * width)
        prm[p, 2] = (1.0 - mixing) * (0.9394373 * inv)
        prm[p, 3] = (-2.7725887 * 1.4426950408889634) * (inv * inv)
        prm[p, 4] = jnp.exp(-(invt * energy))

    def prepare_some(i, _):
        for j in range(PREP):
            prepare(PREP * i + j)
        return 0

    lax.fori_loop(0, lax.div(ends[1] + (PREP - 1), PREP), prepare_some, 0)

    def group(p, far):
        n = 2 * far + BUCKET
        rec = jnp.concatenate([live[GROUP * p + j] for j in range(GROUP)], axis=1)
        center, strength, kind, limit, side = rec[0:1], rec[4:5], rec[5:6], rec[6:7], rec[7:8]
        bucket = jnp.minimum(jnp.floor(center * (1.0 / BUCKET)), NBUCKET - 1.0)
        frac = center - BUCKET * bucket
        hot[...] = jnp.where(bucket_row == bucket + NBUCKET * side, 1.0, 0.0).astype(jnp.bfloat16)
        point = lax.broadcasted_iota(jnp.int32, (n, GROUP * LANES), 0).astype(jnp.float32) - float(far)
        x = point - frac
        sq[0:n] = jnp.where(jnp.abs(x) <= limit, x * x, jnp.inf)

        def at_point(t, _):
            at = pl.ds(t, 1)
            picked = jnp.zeros((8, GROUP * LANES), jnp.float32)
            for s in range(SUB):
                ab = abund[t, s]
                picked = jnp.where(kind == float(s), jnp.concatenate([ab] * GROUP, axis=1), picked)
            w8 = picked * strength * prm[p, 4, at, :]
            w16 = jnp.concatenate([w8, w8], axis=0).astype(jnp.bfloat16)
            wide = hot[...] * jnp.concatenate([w16] * (COLS // 16), axis=0)
            a, b, g, h = [prm[p, j, at, :] for j in range(4)]
            s2 = sq[0:n]
            shape = a * pl.reciprocal(s2 + b, approx=True) + g * jnp.exp2(s2 * h)
            part = lax.dot_general(
                shape.astype(jnp.bfloat16),
                wide,
                (((1,), (1,)), ((), ())),
                preferred_element_type=jnp.float32,
            )
            low = HALO - far
            acc[t, low : low + n, 0:COLS] = acc[t, low : low + n, 0:COLS] + part
            return 0

        lax.fori_loop(0, TP, at_point, 0, unroll=UNROLL)

    for c in range(CLASSES, 0, -1):
        def body(p, _, far=STEP * c):
            group(p, far)
            return 0

        lax.fori_loop(ends[c + 1], ends[c], body, 0)


def fold_kernel(acc, out):
    lane = lax.broadcasted_iota(jnp.int32, (BUCKET, LANES), 1)
    half = (NBUCKET + HALO // BUCKET) * MIXES
    for t in range(TP):
        low = acc[t, 0:BUCKET, :]
        high = jnp.zeros((BUCKET, LANES), jnp.float32)
        for i in range(1, ROWS // BUCKET):
            turned = pltpu.roll(acc[t, BUCKET * i : BUCKET * (i + 1), :], MIXES * i, 1)
            passed = lane < MIXES * i
            low = low + jnp.where(passed, 0.0, turned)
            high = high + jnp.where(passed, turned, 0.0)
        second = jnp.where(lane < LANES - half, pltpu.roll(low, LANES - half, 1), pltpu.roll(high, LANES - half, 1))
        out[t // 2, 0, t % 2] = low
        out[t // 2, 1, t % 2] = second


def opacity(scalars, recs, abund, temps):
    nslots = recs.shape[0]
    groups = PREP * (-(-nslots // (GROUP * PREP)))

    def kernel(scalars, recs, abund, temps, out, acc, *scratch):
        opacity_kernel(nslots, scalars, recs, abund, temps, acc, *scratch)
        fold_kernel(acc, out)

    return pl.pallas_call(
        kernel,
        out_shape=jax.ShapeDtypeStruct((TP // 2, 2, 2, BUCKET, LANES), jnp.float32),
        in_specs=[SMEM, VMEM, VMEM, VMEM],
        out_specs=VMEM,
        scratch_shapes=[
            pltpu.VMEM((TP, ROWS, LANES), jnp.float32),
            pltpu.SMEM((nslots,), jnp.int32),
            pltpu.SMEM((CLASSES + 1,), jnp.int32),
            pltpu.SMEM((CLASSES + 1,), jnp.int32),
            pltpu.VMEM((GROUP * groups + 2, FIELDS, LANES), jnp.float32),
            pltpu.VMEM((groups, 5, TP, GROUP * LANES), jnp.float32),
            pltpu.VMEM((COLS, GROUP * LANES), jnp.bfloat16),
            pltpu.VMEM((ROWS, GROUP * LANES), jnp.float32),
        ],
        compiler_params=pltpu.CompilerParams(vmem_limit_bytes=24 * 2**20),
        name="opacity",
    )(scalars, recs, abund, temps)


def per_device(
    dest_tiles,
    line_counts,
    wing_widths,
    species_ids,
    offsets,
    strengths,
    doppler,
    lorentz,
    energy,
    temp_scale,
    press_scale,
    inverse_temp,
    abundances,
):
    ntiles = lax.axis_size("wave")
    nblocks = dest_tiles.shape[1]

    def rows(array):
        return array.reshape(nblocks, LANES)

    packed = pl.pallas_call(
        lambda *refs: pack_kernel(nblocks, *refs),
        out_shape=jax.ShapeDtypeStruct((2 * ntiles, FIELDS, LANES), jnp.float32),
        in_specs=[SMEM] * 3 + [VMEM] * 6,
        out_specs=VMEM,
        scratch_shapes=[pltpu.SMEM((ntiles,), jnp.int32)],
        name="pack",
    )(
        dest_tiles.reshape(nblocks),
        line_counts.reshape(nblocks),
        wing_widths.reshape(nblocks),
        rows(offsets),
        rows(doppler),
        rows(lorentz),
        rows(energy),
        rows(strengths),
        rows(species_ids),
    )
    cores = [list(range(core, ntiles, 2)) for core in range(2)]
    recs = lax.all_to_all(packed, "wave", split_axis=0, concat_axis=0, tiled=True, axis_index_groups=cores)
    scalars = jnp.transpose(recs[:, 6:8, 0]).astype(jnp.int32)
    abund = jnp.transpose(abundances[:, 0], (2, 1, 0))
    abund = jnp.tile(abund, (1, 1, 2))[..., None] + jnp.zeros((LANES,), jnp.float32)
    temps = jnp.stack([temp_scale, press_scale, inverse_temp], axis=1)
    summed = opacity(scalars, recs, abund, temps)
    groups = lax.axis_size("species")
    chips = [[g * ntiles + first + core for g in range(groups) for core in range(2)] for first in range(0, ntiles, 2)]
    shares = lax.all_to_all(
        summed.reshape(2 * groups, 2, BUCKET, LANES),
        ("species", "wave"),
        split_axis=0,
        concat_axis=0,
        tiled=True,
        axis_index_groups=chips,
    )
    mine = jnp.sum(shares, axis=0)

    odd = lax.axis_index("wave") % 2 == 1
    wing = (HALO // BUCKET) * MIXES
    body = NBUCKET * MIXES
    across = [(i, i + 1) for i in range(1, ntiles - 1, 2)]
    across = across + [(i + 1, i) for i in range(1, ntiles - 1, 2)]
    sent = jnp.where(odd, mine[:, :, body : body + wing], mine[:, :, :wing])
    got = lax.ppermute(sent, "wave", across)
    outer = ((0, 0), (0, 0))
    near = jnp.pad(got, outer + ((0, body - wing),))
    far = jnp.pad(got, outer + ((body - wing, 0),))
    middle = jnp.where(odd, mine[:, :, :body] + far, mine[:, :, wing : wing + body] + near)
    middle = middle.reshape(-1, BUCKET, NBUCKET, MIXES)
    return jnp.transpose(middle, (3, 0, 2, 1)).reshape(MIXES, -1, TILE)


def solution(mesh):
    line = P("species", "wave")
    return jax.shard_map(
        per_device,
        mesh=mesh,
        in_specs=(P("species", "wave", None),) + (line,) * 8 + (P(), P(), P(), P(None, "species", None, None)),
        out_specs=P(None, "species", "wave"),
        check_vma=False,
    )
```

```python
import jax
import jax.numpy as jnp
from jax import lax
from jax.experimental import pallas as pl
from jax.experimental.pallas import tpu as pltpu
from jax.sharding import PartitionSpec as P

TILE = 256
TP = 16
MIXES = 4
SUB = 4
HALO = 64
LANES = 128
FIELDS = 8
BUCKET = 16
NBUCKET = TILE // BUCKET
ROWS = 2 * HALO + BUCKET
COLS = 2 * NBUCKET * MIXES
STEP = 8
CLASSES = HALO // STEP
UNROLL = 16
GROUP = 4
PREP = 2
POUR = 4

VMEM = pl.BlockSpec(memory_space=pltpu.VMEM)
SMEM = pl.BlockSpec(memory_space=pltpu.SMEM)


def pack_kernel(nblocks, dest, counts, reach, off, dop, lor, ene, stre, spec, out, used):
    ntiles = used.shape[0]
    empty = jnp.zeros((FIELDS, LANES), jnp.float32)

    def clear(tile, _):
        used[tile] = 0
        out[2 * tile] = empty
        out[2 * tile + 1] = empty
        return 0

    lax.fori_loop(0, ntiles, clear, 0, unroll=4)

    def place(block, _):
        tile = dest[block]
        rank = used[tile]
        used[tile] = rank + 1
        slot = 2 * tile + rank
        at = pl.ds(block, 1)
        out[slot, 0:1, :] = off[at, :]
        out[slot, 1:2, :] = dop[at, :]
        out[slot, 2:3, :] = lor[at, :]
        out[slot, 3:4, :] = ene[at, :]
        out[slot, 4:5, :] = stre[at, :]
        out[slot, 5:6, :] = spec[at, :].astype(jnp.float32)
        out[slot, 6:7, :] = jnp.full((1, LANES), reach[block].astype(jnp.float32))
        out[slot, 7:8, :] = jnp.full((1, LANES), counts[block].astype(jnp.float32))
        return 0

    lax.fori_loop(0, nblocks, place, 0, unroll=4)


def opacity_kernel(nslots, scalars, recs, abund, temps, acc, order, first, lines, live, prm, hot, sq):
    def klass(i):
        wing = scalars[0, i]
        c = jnp.minimum(lax.shift_right_logical(wing, 3) + 1, CLASSES)
        return jnp.where(wing > 0, c, 0)

    def count(i, _):
        c = klass(i)
        first[c] = first[c] + 1
        lines[c] = lines[c] + scalars[1, i]
        return 0

    for c in range(CLASSES + 1):
        first[c] = 0
        lines[c] = 0
    lax.fori_loop(0, nslots, count, 0, unroll=8)
    slots, total = jnp.int32(0), jnp.int32(0)
    ends = {CLASSES + 1: total}
    for c in range(CLASSES, 0, -1):
        held = first[c]
        first[c] = slots
        slots = slots + held
        total = total + lines[c]
        ends[c] = lax.div(total + (GROUP * LANES - 1), GROUP * LANES)
    first[0] = slots

    def place(i, _):
        c = klass(i)
        at = first[c]
        order[at] = i
        first[c] = at + 1
        return 0

    lax.fori_loop(0, nslots, place, 0, unroll=8)

    row = lax.broadcasted_iota(jnp.int32, (FIELDS, LANES), 0)
    lane = lax.broadcasted_iota(jnp.int32, (FIELDS, LANES), 1)
    blank = jnp.where((row == 1) | (row == 2), 1.0, 0.0)

    def empty(i, _):
        live[i] = blank
        return 0

    lax.fori_loop(0, live.shape[0], empty, 0, unroll=6)

    def pour(i, filled):
        for j in range(POUR):
            slot = order[POUR * i + j]
            held = scalars[1, slot]
            into = lax.shift_right_logical(filled, 7)
            turn = lax.bitwise_and(filled, LANES - 1)
            side = lax.bitwise_and(lax.shift_right_logical(slot, 1), 1)
            record = jnp.where(row == 7, side.astype(jnp.float32), recs[slot])
            turned = pltpu.roll(record, turn, 1)
            pltpu.store(live.at[into], turned, mask=(lane >= turn) & (lane < turn + held))
            pltpu.store(live.at[into + 1], turned, mask=lane < turn + held - LANES)
            filled = filled + held
        return filled

    lax.fori_loop(0, lax.div(slots + (POUR - 1), POUR), pour, jnp.int32(0))

    def wipe(t, _):
        acc[t] = jnp.zeros(acc.shape[1:], jnp.float32)
        return 0

    lax.fori_loop(0, TP, wipe, 0)

    tscale, pscale, invt = temps[:, 0:1], temps[:, 1:2], temps[:, 2:3]
    bucket_row = lax.shift_right_logical(lax.broadcasted_iota(jnp.int32, (COLS, GROUP * LANES), 0), 2)
    bucket_row = bucket_row.astype(jnp.float32)

    def prepare(p):
        rec = jnp.concatenate([live[GROUP * p + j] for j in range(GROUP)], axis=1)
        dop, lor, energy = rec[1:2], rec[2:3], rec[3:4]
        gauss = 2.35482 * (tscale * dop)
        lorz = 2.0 * (pscale * lor)
        g2, l2 = gauss * gauss, lorz * lorz
        g4, l4 = g2 * g2, l2 * l2
        fifth = (
            g4 * gauss
            + 2.69269 * g4 * lorz
            + 2.42843 * (g2 * gauss) * l2
            + 4.47163 * g2 * (l2 * lorz)
            + 0.07842 * gauss * l4
            + l4 * lorz
        )
        width = jnp.exp(0.2 * jnp.log(fifth))
        inv = 1.0 / width
        q = lorz * inv
        mixing = q * (1.36603 + q * (-0.47719 + q * 0.11116))
        prm[p, 0] = mixing * (0.15915494 * width)
        prm[p, 1] = 0.25 * (width * width)
        prm[p, 2] = (1.0 - mixing) * (0.9394373 * inv)
        prm[p, 3] = (-2.7725887 * 1.4426950408889634) * (inv * inv)
        prm[p, 4] = jnp.exp(-(invt * energy))

    def prepare_some(i, _):
        for j in range(PREP):
            prepare(PREP * i + j)
        return 0

    lax.fori_loop(0, lax.div(ends[1] + (PREP - 1), PREP), prepare_some, 0)

    def group(p, far):
        n = 2 * far + BUCKET
        rec = jnp.concatenate([live[GROUP * p + j] for j in range(GROUP)], axis=1)
        center, strength, kind, limit, side = rec[0:1], rec[4:5], rec[5:6], rec[6:7], rec[7:8]
        bucket = jnp.minimum(jnp.floor(center * (1.0 / BUCKET)), NBUCKET - 1.0)
        frac = center - BUCKET * bucket
        hot[...] = jnp.where(bucket_row == bucket + NBUCKET * side, 1.0, 0.0).astype(jnp.bfloat16)
        point = lax.broadcasted_iota(jnp.int32, (n, GROUP * LANES), 0).astype(jnp.float32) - float(far)
        x = point - frac
        sq[0:n] = jnp.where(jnp.abs(x) <= limit, x * x, jnp.inf)

        def at_point(t, _):
            at = pl.ds(t, 1)
            picked = jnp.zeros((8, GROUP * LANES), jnp.float32)
            for s in range(SUB):
                ab = abund[t, s]
                picked = jnp.where(kind == float(s), jnp.concatenate([ab] * GROUP, axis=1), picked)
            w8 = picked * strength * prm[p, 4, at, :]
            w16 = jnp.concatenate([w8, w8], axis=0).astype(jnp.bfloat16)
            wide = hot[...] * jnp.concatenate([w16] * (COLS // 16), axis=0)
            a, b, g, h = [prm[p, j, at, :] for j in range(4)]
            s2 = sq[0:n]
            shape = a * pl.reciprocal(s2 + b, approx=True) + g * jnp.exp2(s2 * h)
            part = lax.dot_general(
                shape.astype(jnp.bfloat16),
                wide,
                (((1,), (1,)), ((), ())),
                preferred_element_type=jnp.float32,
            )
            low = HALO - far
            acc[t, low : low + n, 0:COLS] = acc[t, low : low + n, 0:COLS] + part
            return 0

        lax.fori_loop(0, TP, at_point, 0, unroll=UNROLL)

    for c in range(CLASSES, 0, -1):
        def body(p, _, far=STEP * c):
            group(p, far)
            return 0

        lax.fori_loop(ends[c + 1], ends[c], body, 0)


def fold_kernel(core, acc, own, other):
    lane = lax.broadcasted_iota(jnp.int32, (BUCKET, LANES), 1)
    body, wing = NBUCKET * MIXES, (HALO // BUCKET) * MIXES
    half = body + wing
    for t in range(TP):
        low = acc[t, 0:BUCKET, :]
        high = jnp.zeros((BUCKET, LANES), jnp.float32)
        for i in range(1, ROWS // BUCKET):
            turned = pltpu.roll(acc[t, BUCKET * i : BUCKET * (i + 1), :], MIXES * i, 1)
            passed = lane < MIXES * i
            low = low + jnp.where(passed, 0.0, turned)
            high = high + jnp.where(passed, turned, 0.0)
        second = jnp.where(lane < LANES - half, pltpu.roll(low, LANES - half, 1), pltpu.roll(high, LANES - half, 1))
        first = jnp.where((lane < body) | (lane >= LANES - wing), pltpu.roll(low, LANES - wing, 1), 0.0)
        own[t] = jnp.where(core == 0, first, second)
        other[t] = jnp.where(core == 0, second, first)


def opacity(core, scalars, recs, abund, temps):
    nslots = recs.shape[0]
    groups = PREP * (-(-nslots // (GROUP * PREP)))

    def kernel(core, scalars, recs, abund, temps, own, other, acc, *scratch):
        opacity_kernel(nslots, scalars, recs, abund, temps, acc, *scratch)
        fold_kernel(core[0], acc, own, other)

    return pl.pallas_call(
        kernel,
        out_shape=[jax.ShapeDtypeStruct((TP, BUCKET, LANES), jnp.float32)] * 2,
        in_specs=[SMEM, SMEM, VMEM, VMEM, VMEM],
        out_specs=[VMEM, VMEM],
        scratch_shapes=[
            pltpu.VMEM((TP, ROWS, LANES), jnp.float32),
            pltpu.SMEM((nslots,), jnp.int32),
            pltpu.SMEM((CLASSES + 1,), jnp.int32),
            pltpu.SMEM((CLASSES + 1,), jnp.int32),
            pltpu.VMEM((GROUP * groups + 2, FIELDS, LANES), jnp.float32),
            pltpu.VMEM((groups, 5, TP, GROUP * LANES), jnp.float32),
            pltpu.VMEM((COLS, GROUP * LANES), jnp.bfloat16),
            pltpu.VMEM((ROWS, GROUP * LANES), jnp.float32),
        ],
        compiler_params=pltpu.CompilerParams(vmem_limit_bytes=24 * 2**20),
        name="opacity",
    )(core, scalars, recs, abund, temps)


def per_device(
    dest_tiles,
    line_counts,
    wing_widths,
    species_ids,
    offsets,
    strengths,
    doppler,
    lorentz,
    energy,
    temp_scale,
    press_scale,
    inverse_temp,
    abundances,
):
    ntiles = lax.axis_size("wave")
    nblocks = dest_tiles.shape[1]

    def rows(array):
        return array.reshape(nblocks, LANES)

    packed = pl.pallas_call(
        lambda *refs: pack_kernel(nblocks, *refs),
        out_shape=jax.ShapeDtypeStruct((2 * ntiles, FIELDS, LANES), jnp.float32),
        in_specs=[SMEM] * 3 + [VMEM] * 6,
        out_specs=VMEM,
        scratch_shapes=[pltpu.SMEM((ntiles,), jnp.int32)],
        name="pack",
    )(
        dest_tiles.reshape(nblocks),
        line_counts.reshape(nblocks),
        wing_widths.reshape(nblocks),
        rows(offsets),
        rows(doppler),
        rows(lorentz),
        rows(energy),
        rows(strengths),
        rows(species_ids),
    )
    cores = [list(range(core, ntiles, 2)) for core in range(2)]
    recs = lax.all_to_all(packed, "wave", split_axis=0, concat_axis=0, tiled=True, axis_index_groups=cores)
    scalars = jnp.transpose(recs[:, 6:8, 0]).astype(jnp.int32)
    abund = jnp.transpose(abundances[:, 0], (2, 1, 0))
    abund = jnp.tile(abund, (1, 1, 2))[..., None] + jnp.zeros((LANES,), jnp.float32)
    temps = jnp.stack([temp_scale, press_scale, inverse_temp], axis=1)
    core = lax.axis_index("wave") % 2
    own, other = opacity(core.reshape(1), scalars, recs, abund, temps)
    twin = lax.ppermute(other, "wave", [(i, i ^ 1) for i in range(ntiles)])
    shares = lax.all_to_all(own + twin, "species", split_axis=0, concat_axis=0, tiled=True)
    mine = jnp.sum(shares.reshape(-1, TP // lax.axis_size("species"), BUCKET, LANES), axis=0)

    body = NBUCKET * MIXES
    across = [(i, i + 1) for i in range(1, ntiles - 1, 2)]
    across = across + [(i + 1, i) for i in range(1, ntiles - 1, 2)]
    middle = mine[:, :, :body] + lax.ppermute(mine[:, :, body:], "wave", across)
    middle = middle.reshape(-1, BUCKET, NBUCKET, MIXES)
    return jnp.transpose(middle, (3, 0, 2, 1)).reshape(MIXES, -1, TILE)


def solution(mesh):
    line = P("species", "wave")
    return jax.shard_map(
        per_device,
        mesh=mesh,
        in_specs=(P("species", "wave", None),) + (line,) * 8 + (P(), P(), P(), P(None, "species", None, None)),
        out_specs=P(None, "species", "wave"),
        check_vma=False,
    )
```

```python
import jax
import jax.numpy as jnp
from jax import lax
from jax.experimental import pallas as pl
from jax.experimental.pallas import tpu as pltpu
from jax.sharding import PartitionSpec as P

TILE = 256
TP = 16
MIXES = 4
SUB = 4
HALO = 64
LANES = 128
FIELDS = 8
BUCKET = 16
NBUCKET = TILE // BUCKET
ROWS = 2 * HALO + BUCKET
COLS = 2 * NBUCKET * MIXES
STEP = 8
CLASSES = HALO // STEP
UNROLL = 16
GROUP = 4
PREP = 2
POUR = 4

VMEM = pl.BlockSpec(memory_space=pltpu.VMEM)
SMEM = pl.BlockSpec(memory_space=pltpu.SMEM)


def tables_kernel(abundance, temp, press, invtemp, tables):
    at = lax.broadcasted_iota(jnp.int32, (TP, LANES), 0)
    for which, values in enumerate((temp, press, invtemp)):
        made = jnp.zeros((TP, LANES), jnp.float32)
        for t in range(TP):
            made = jnp.where(at == t, values[t], made)
        tables[TP * SUB + 2 * which] = made[:FIELDS]
        tables[TP * SUB + 2 * which + 1] = made[FIELDS:]
    mix = lax.bitwise_and(lax.broadcasted_iota(jnp.int32, (FIELDS, LANES), 0), MIXES - 1)

    def spread(t, _):
        for s in range(SUB):
            made = jnp.zeros((FIELDS, LANES), jnp.float32)
            for m in range(MIXES):
                made = jnp.where(mix == m, abundance[m, 0, s, t], made)
            tables[t * SUB + s] = made
        return 0

    lax.fori_loop(0, TP, spread, 0, unroll=4)


def pack_kernel(nblocks, dest, counts, reach, off, dop, lor, ene, stre, spec, out, used):
    ntiles = used.shape[0]
    empty = jnp.zeros((FIELDS, LANES), jnp.float32)

    def clear(tile, _):
        used[tile] = 0
        out[2 * tile] = empty
        out[2 * tile + 1] = empty
        return 0

    lax.fori_loop(0, ntiles, clear, 0, unroll=4)

    def place(block, _):
        tile = dest[block]
        rank = used[tile]
        used[tile] = rank + 1
        slot = 2 * tile + rank
        at = pl.ds(block, 1)
        out[slot, 0:1, :] = off[at, :]
        out[slot, 1:2, :] = dop[at, :]
        out[slot, 2:3, :] = lor[at, :]
        out[slot, 3:4, :] = ene[at, :]
        out[slot, 4:5, :] = stre[at, :]
        out[slot, 5:6, :] = spec[at, :].astype(jnp.float32)
        out[slot, 6:7, :] = jnp.full((1, LANES), reach[block].astype(jnp.float32))
        out[slot, 7:8, :] = jnp.full((1, LANES), counts[block].astype(jnp.float32))
        return 0

    lax.fori_loop(0, nblocks, place, 0, unroll=4)


def opacity_kernel(nslots, scalars, recs, tables, acc, order, first, lines, live, prm, hot, sq):
    def klass(i):
        wing = scalars[0, i]
        c = jnp.minimum(lax.shift_right_logical(wing, 3) + 1, CLASSES)
        return jnp.where(wing > 0, c, 0)

    def count(i, _):
        c = klass(i)
        first[c] = first[c] + 1
        lines[c] = lines[c] + scalars[1, i]
        return 0

    for c in range(CLASSES + 1):
        first[c] = 0
        lines[c] = 0
    lax.fori_loop(0, nslots, count, 0, unroll=8)
    slots, total = jnp.int32(0), jnp.int32(0)
    ends = {CLASSES + 1: total}
    for c in range(CLASSES, 0, -1):
        held = first[c]
        first[c] = slots
        slots = slots + held
        total = total + lines[c]
        ends[c] = lax.div(total + (GROUP * LANES - 1), GROUP * LANES)
    first[0] = slots

    def place(i, _):
        c = klass(i)
        at = first[c]
        order[at] = i
        first[c] = at + 1
        return 0

    lax.fori_loop(0, nslots, place, 0, unroll=8)

    row = lax.broadcasted_iota(jnp.int32, (FIELDS, LANES), 0)
    lane = lax.broadcasted_iota(jnp.int32, (FIELDS, LANES), 1)
    blank = jnp.where((row == 1) | (row == 2), 1.0, 0.0)

    def empty(i, _):
        live[i] = blank
        return 0

    lax.fori_loop(0, live.shape[0], empty, 0, unroll=6)

    def pour(i, filled):
        for j in range(POUR):
            slot = order[POUR * i + j]
            held = scalars[1, slot]
            into = lax.shift_right_logical(filled, 7)
            turn = lax.bitwise_and(filled, LANES - 1)
            side = lax.bitwise_and(lax.shift_right_logical(slot, 1), 1)
            record = jnp.where(row == 7, side.astype(jnp.float32), recs[slot])
            turned = pltpu.roll(record, turn, 1)
            pltpu.store(live.at[into], turned, mask=(lane >= turn) & (lane < turn + held))
            pltpu.store(live.at[into + 1], turned, mask=lane < turn + held - LANES)
            filled = filled + held
        return filled

    lax.fori_loop(0, lax.div(slots + (POUR - 1), POUR), pour, jnp.int32(0))

    def wipe(t, _):
        acc[t] = jnp.zeros(acc.shape[1:], jnp.float32)
        return 0

    lax.fori_loop(0, TP, wipe, 0)

    def column(which):
        made = jnp.concatenate([tables[TP * SUB + 2 * which], tables[TP * SUB + 2 * which + 1]], axis=0)
        return jnp.concatenate([made] * GROUP, axis=1)

    tscale, pscale, invt = column(0), column(1), column(2)
    bucket_row = lax.shift_right_logical(lax.broadcasted_iota(jnp.int32, (COLS, GROUP * LANES), 0), 2)
    bucket_row = bucket_row.astype(jnp.float32)

    def prepare(p):
        rec = jnp.concatenate([live[GROUP * p + j] for j in range(GROUP)], axis=1)
        dop, lor, energy = rec[1:2], rec[2:3], rec[3:4]
        gauss = 2.35482 * (tscale * dop)
        lorz = 2.0 * (pscale * lor)
        g2, l2 = gauss * gauss, lorz * lorz
        g4, l4 = g2 * g2, l2 * l2
        fifth = (
            g4 * gauss
            + 2.69269 * g4 * lorz
            + 2.42843 * (g2 * gauss) * l2
            + 4.47163 * g2 * (l2 * lorz)
            + 0.07842 * gauss * l4
            + l4 * lorz
        )
        width = jnp.exp(0.2 * jnp.log(fifth))
        inv = 1.0 / width
        q = lorz * inv
        mixing = q * (1.36603 + q * (-0.47719 + q * 0.11116))
        prm[p, 0] = mixing * (0.15915494 * width)
        prm[p, 1] = 0.25 * (width * width)
        prm[p, 2] = (1.0 - mixing) * (0.9394373 * inv)
        prm[p, 3] = (-2.7725887 * 1.4426950408889634) * (inv * inv)
        prm[p, 4] = jnp.exp(-(invt * energy))

    def prepare_some(i, _):
        for j in range(PREP):
            prepare(PREP * i + j)
        return 0

    lax.fori_loop(0, lax.div(ends[1] + (PREP - 1), PREP), prepare_some, 0)

    def group(p, far):
        n = 2 * far + BUCKET
        rec = jnp.concatenate([live[GROUP * p + j] for j in range(GROUP)], axis=1)
        center, strength, kind, limit, side = rec[0:1], rec[4:5], rec[5:6], rec[6:7], rec[7:8]
        bucket = jnp.minimum(jnp.floor(center * (1.0 / BUCKET)), NBUCKET - 1.0)
        frac = center - BUCKET * bucket
        hot[...] = jnp.where(bucket_row == bucket + NBUCKET * side, 1.0, 0.0).astype(jnp.bfloat16)
        point = lax.broadcasted_iota(jnp.int32, (n, GROUP * LANES), 0).astype(jnp.float32) - float(far)
        x = point - frac
        sq[0:n] = jnp.where(jnp.abs(x) <= limit, x * x, jnp.inf)

        def at_point(t, _):
            at = pl.ds(t, 1)
            picked = jnp.zeros((8, GROUP * LANES), jnp.float32)
            for s in range(SUB):
                ab = tables[t * SUB + s]
                picked = jnp.where(kind == float(s), jnp.concatenate([ab] * GROUP, axis=1), picked)
            w8 = picked * strength * prm[p, 4, at, :]
            w16 = jnp.concatenate([w8, w8], axis=0).astype(jnp.bfloat16)
            wide = hot[...] * jnp.concatenate([w16] * (COLS // 16), axis=0)
            a, b, g, h = [prm[p, j, at, :] for j in range(4)]
            s2 = sq[0:n]
            shape = a * pl.reciprocal(s2 + b, approx=True) + g * jnp.exp2(s2 * h)
            part = lax.dot_general(
                shape.astype(jnp.bfloat16),
                wide,
                (((1,), (1,)), ((), ())),
                preferred_element_type=jnp.float32,
            )
            low = HALO - far
            acc[t, low : low + n, 0:COLS] = acc[t, low : low + n, 0:COLS] + part
            return 0

        lax.fori_loop(0, TP, at_point, 0, unroll=UNROLL)

    for c in range(CLASSES, 0, -1):
        def body(p, _, far=STEP * c):
            group(p, far)
            return 0

        lax.fori_loop(ends[c + 1], ends[c], body, 0)


def fold_kernel(core, acc, own, other):
    lane = lax.broadcasted_iota(jnp.int32, (BUCKET, LANES), 1)
    body, wing = NBUCKET * MIXES, (HALO // BUCKET) * MIXES
    half = body + wing
    for t in range(TP):
        low = acc[t, 0:BUCKET, :]
        high = jnp.zeros((BUCKET, LANES), jnp.float32)
        for i in range(1, ROWS // BUCKET):
            turned = pltpu.roll(acc[t, BUCKET * i : BUCKET * (i + 1), :], MIXES * i, 1)
            passed = lane < MIXES * i
            low = low + jnp.where(passed, 0.0, turned)
            high = high + jnp.where(passed, turned, 0.0)
        second = jnp.where(lane < LANES - half, pltpu.roll(low, LANES - half, 1), pltpu.roll(high, LANES - half, 1))
        first = jnp.where((lane < body) | (lane >= LANES - wing), pltpu.roll(low, LANES - wing, 1), 0.0)
        own[t] = jnp.where(core == 0, first, second)
        other[t] = jnp.where(core == 0, second, first)


def core_number():
    return lax.rem(lax.axis_index("wave"), 2)


def opacity(scalars, recs, tables):
    nslots = recs.shape[0]
    groups = PREP * (-(-nslots // (GROUP * PREP)))

    def kernel(scalars, recs, tables, own, other, acc, *scratch):
        opacity_kernel(nslots, scalars, recs, tables, acc, *scratch)
        fold_kernel(core_number(), acc, own, other)

    return pl.pallas_call(
        kernel,
        out_shape=[jax.ShapeDtypeStruct((TP, BUCKET, LANES), jnp.float32)] * 2,
        in_specs=[SMEM, VMEM, VMEM],
        out_specs=[VMEM, VMEM],
        scratch_shapes=[
            pltpu.VMEM((TP, ROWS, LANES), jnp.float32),
            pltpu.SMEM((nslots,), jnp.int32),
            pltpu.SMEM((CLASSES + 1,), jnp.int32),
            pltpu.SMEM((CLASSES + 1,), jnp.int32),
            pltpu.VMEM((GROUP * groups + 2, FIELDS, LANES), jnp.float32),
            pltpu.VMEM((groups, 5, TP, GROUP * LANES), jnp.float32),
            pltpu.VMEM((COLS, GROUP * LANES), jnp.bfloat16),
            pltpu.VMEM((ROWS, GROUP * LANES), jnp.float32),
        ],
        compiler_params=pltpu.CompilerParams(vmem_limit_bytes=24 * 2**20),
        name="opacity",
    )(scalars, recs, tables)


def per_device(
    dest_tiles,
    line_counts,
    wing_widths,
    species_ids,
    offsets,
    strengths,
    doppler,
    lorentz,
    energy,
    temp_scale,
    press_scale,
    inverse_temp,
    abundances,
):
    ntiles = lax.axis_size("wave")
    nblocks = dest_tiles.shape[1]

    def rows(array):
        return array.reshape(nblocks, LANES)

    def kernel(*refs):
        tables_kernel(*refs[9:13], refs[14])
        pack_kernel(nblocks, *refs[:9], refs[13], refs[15])

    packed, tables = pl.pallas_call(
        kernel,
        out_shape=[
            jax.ShapeDtypeStruct((2 * ntiles, FIELDS, LANES), jnp.float32),
            jax.ShapeDtypeStruct((TP * SUB + 6, FIELDS, LANES), jnp.float32),
        ],
        in_specs=[SMEM] * 3 + [VMEM] * 6 + [SMEM] * 4,
        out_specs=[VMEM] * 2,
        scratch_shapes=[pltpu.SMEM((ntiles,), jnp.int32)],
        name="pack",
    )(
        dest_tiles.reshape(nblocks),
        line_counts.reshape(nblocks),
        wing_widths.reshape(nblocks),
        rows(offsets),
        rows(doppler),
        rows(lorentz),
        rows(energy),
        rows(strengths),
        rows(species_ids),
        abundances,
        temp_scale,
        press_scale,
        inverse_temp,
    )
    cores = [list(range(core, ntiles, 2)) for core in range(2)]
    recs = lax.all_to_all(packed, "wave", split_axis=0, concat_axis=0, tiled=True, axis_index_groups=cores)
    scalars = jnp.transpose(recs[:, 6:8, 0]).astype(jnp.int32)
    own, other = opacity(scalars, recs, tables)
    twin = lax.ppermute(other, "wave", [(i, i ^ 1) for i in range(ntiles)])
    shares = lax.all_to_all(own + twin, "species", split_axis=0, concat_axis=0, tiled=True)
    mine = jnp.sum(shares.reshape(-1, TP // lax.axis_size("species"), BUCKET, LANES), axis=0)

    body = NBUCKET * MIXES
    across = [(i, i + 1) for i in range(1, ntiles - 1, 2)]
    across = across + [(i + 1, i) for i in range(1, ntiles - 1, 2)]
    middle = mine[:, :, :body] + lax.ppermute(mine[:, :, body:], "wave", across)
    middle = middle.reshape(-1, BUCKET, NBUCKET, MIXES)
    return jnp.transpose(middle, (3, 0, 2, 1)).reshape(MIXES, -1, TILE)


def solution(mesh):
    line = P("species", "wave")
    return jax.shard_map(
        per_device,
        mesh=mesh,
        in_specs=(P("species", "wave", None),) + (line,) * 8 + (P(), P(), P(), P(None, "species", None, None)),
        out_specs=P(None, "species", "wave"),
        check_vma=False,
    )
```

```python
import jax
import jax.numpy as jnp
from jax import lax
from jax.experimental import pallas as pl
from jax.experimental.pallas import tpu as pltpu
from jax.sharding import PartitionSpec as P

TILE = 256
TP = 16
MIXES = 4
SUB = 4
HALO = 64
LANES = 128
FIELDS = 8
BUCKET = 16
NBUCKET = TILE // BUCKET
ROWS = 2 * HALO + BUCKET
COLS = 2 * NBUCKET * MIXES
STEP = 8
CLASSES = HALO // STEP
UNROLL = 16
GROUP = 4
PREP = 2
POUR = 8

VMEM = pl.BlockSpec(memory_space=pltpu.VMEM)
SMEM = pl.BlockSpec(memory_space=pltpu.SMEM)


def tables_kernel(abundance, temp, press, invtemp, tables):
    at = lax.broadcasted_iota(jnp.int32, (TP, LANES), 0)
    for which, values in enumerate((temp, press, invtemp)):
        made = jnp.zeros((TP, LANES), jnp.float32)
        for t in range(TP):
            made = jnp.where(at == t, values[t], made)
        tables[TP * SUB + 2 * which] = made[:FIELDS]
        tables[TP * SUB + 2 * which + 1] = made[FIELDS:]
    mix = lax.bitwise_and(lax.broadcasted_iota(jnp.int32, (FIELDS, LANES), 0), MIXES - 1)

    def spread(t, _):
        for s in range(SUB):
            made = jnp.zeros((FIELDS, LANES), jnp.float32)
            for m in range(MIXES):
                made = jnp.where(mix == m, abundance[m, 0, s, t], made)
            tables[t * SUB + s] = made
        return 0

    lax.fori_loop(0, TP, spread, 0, unroll=16)


def pack_kernel(nblocks, dest, counts, reach, off, dop, lor, ene, stre, spec, out, used):
    ntiles = used.shape[0]
    empty = jnp.zeros((FIELDS, LANES), jnp.float32)

    def clear(tile, _):
        used[tile] = 0
        out[2 * tile] = empty
        out[2 * tile + 1] = empty
        return 0

    lax.fori_loop(0, ntiles, clear, 0, unroll=4)

    def place(block, _):
        tile = dest[block]
        rank = used[tile]
        used[tile] = rank + 1
        slot = 2 * tile + rank
        at = pl.ds(block, 1)
        out[slot, 0:1, :] = off[at, :]
        out[slot, 1:2, :] = dop[at, :]
        out[slot, 2:3, :] = lor[at, :]
        out[slot, 3:4, :] = ene[at, :]
        out[slot, 4:5, :] = stre[at, :]
        out[slot, 5:6, :] = spec[at, :].astype(jnp.float32)
        out[slot, 6:7, :] = jnp.full((1, LANES), reach[block].astype(jnp.float32))
        out[slot, 7:8, :] = jnp.full((1, LANES), counts[block].astype(jnp.float32))
        return 0

    lax.fori_loop(0, nblocks, place, 0, unroll=4)


def opacity_kernel(nslots, scalars, recs, tables, acc, order, first, lines, live, prm, hot, sq):
    def klass(i):
        wing = scalars[0, i]
        c = jnp.minimum(lax.shift_right_logical(wing, 3) + 1, CLASSES)
        return jnp.where(wing > 0, c, 0)

    def count(i, _):
        c = klass(i)
        first[c] = first[c] + 1
        lines[c] = lines[c] + scalars[1, i]
        return 0

    for c in range(CLASSES + 1):
        first[c] = 0
        lines[c] = 0
    lax.fori_loop(0, nslots, count, 0, unroll=8)
    slots, total = jnp.int32(0), jnp.int32(0)
    ends = {CLASSES + 1: total}
    for c in range(CLASSES, 0, -1):
        held = first[c]
        first[c] = slots
        slots = slots + held
        total = total + lines[c]
        ends[c] = lax.div(total + (GROUP * LANES - 1), GROUP * LANES)
    first[0] = slots

    def place(i, _):
        c = klass(i)
        at = first[c]
        order[at] = i
        first[c] = at + 1
        return 0

    lax.fori_loop(0, nslots, place, 0, unroll=8)

    row = lax.broadcasted_iota(jnp.int32, (FIELDS, LANES), 0)
    lane = lax.broadcasted_iota(jnp.int32, (FIELDS, LANES), 1)
    blank = jnp.where((row == 1) | (row == 2), 1.0, 0.0)

    def empty(i, _):
        live[i] = blank
        return 0

    lax.fori_loop(0, live.shape[0], empty, 0, unroll=6)

    def pour(i, filled):
        for j in range(POUR):
            slot = order[POUR * i + j]
            held = scalars[1, slot]
            into = lax.shift_right_logical(filled, 7)
            turn = lax.bitwise_and(filled, LANES - 1)
            side = lax.bitwise_and(lax.shift_right_logical(slot, 1), 1)
            record = jnp.where(row == 7, side.astype(jnp.float32), recs[slot])
            turned = pltpu.roll(record, turn, 1)
            pltpu.store(live.at[into], turned, mask=(lane >= turn) & (lane < turn + held))
            pltpu.store(live.at[into + 1], turned, mask=lane < turn + held - LANES)
            filled = filled + held
        return filled

    lax.fori_loop(0, lax.div(slots + (POUR - 1), POUR), pour, jnp.int32(0))

    def wipe(t, _):
        acc[t] = jnp.zeros(acc.shape[1:], jnp.float32)
        return 0

    lax.fori_loop(0, TP, wipe, 0)

    def column(which):
        made = jnp.concatenate([tables[TP * SUB + 2 * which], tables[TP * SUB + 2 * which + 1]], axis=0)
        return jnp.concatenate([made] * GROUP, axis=1)

    tscale, pscale, invt = column(0), column(1), column(2)
    bucket_row = lax.shift_right_logical(lax.broadcasted_iota(jnp.int32, (COLS, GROUP * LANES), 0), 2)
    bucket_row = bucket_row.astype(jnp.float32)

    def prepare(p):
        rec = jnp.concatenate([live[GROUP * p + j] for j in range(GROUP)], axis=1)
        dop, lor, energy = rec[1:2], rec[2:3], rec[3:4]
        gauss = 2.35482 * (tscale * dop)
        lorz = 2.0 * (pscale * lor)
        g2, l2 = gauss * gauss, lorz * lorz
        g4, l4 = g2 * g2, l2 * l2
        fifth = (
            g4 * gauss
            + 2.69269 * g4 * lorz
            + 2.42843 * (g2 * gauss) * l2
            + 4.47163 * g2 * (l2 * lorz)
            + 0.07842 * gauss * l4
            + l4 * lorz
        )
        width = jnp.exp(0.2 * jnp.log(fifth))
        inv = 1.0 / width
        q = lorz * inv
        mixing = q * (1.36603 + q * (-0.47719 + q * 0.11116))
        prm[p, 0] = mixing * (0.15915494 * width)
        prm[p, 1] = 0.25 * (width * width)
        prm[p, 2] = (1.0 - mixing) * (0.9394373 * inv)
        prm[p, 3] = (-2.7725887 * 1.4426950408889634) * (inv * inv)
        prm[p, 4] = jnp.exp(-(invt * energy))

    def prepare_some(i, _):
        for j in range(PREP):
            prepare(PREP * i + j)
        return 0

    lax.fori_loop(0, lax.div(ends[1] + (PREP - 1), PREP), prepare_some, 0)

    def group(p, far):
        n = 2 * far + BUCKET
        rec = jnp.concatenate([live[GROUP * p + j] for j in range(GROUP)], axis=1)
        center, strength, kind, limit, side = rec[0:1], rec[4:5], rec[5:6], rec[6:7], rec[7:8]
        bucket = jnp.minimum(jnp.floor(center * (1.0 / BUCKET)), NBUCKET - 1.0)
        frac = center - BUCKET * bucket
        hot[...] = jnp.where(bucket_row == bucket + NBUCKET * side, 1.0, 0.0).astype(jnp.bfloat16)
        point = lax.broadcasted_iota(jnp.int32, (n, GROUP * LANES), 0).astype(jnp.float32) - float(far)
        x = point - frac
        sq[0:n] = jnp.where(jnp.abs(x) <= limit, x * x, jnp.inf)

        def at_point(t, _):
            at = pl.ds(t, 1)
            picked = jnp.zeros((8, GROUP * LANES), jnp.float32)
            for s in range(SUB):
                ab = tables[t * SUB + s]
                picked = jnp.where(kind == float(s), jnp.concatenate([ab] * GROUP, axis=1), picked)
            w8 = picked * strength * prm[p, 4, at, :]
            w16 = jnp.concatenate([w8, w8], axis=0).astype(jnp.bfloat16)
            wide = hot[...] * jnp.concatenate([w16] * (COLS // 16), axis=0)
            a, b, g, h = [prm[p, j, at, :] for j in range(4)]
            s2 = sq[0:n]
            shape = a * pl.reciprocal(s2 + b, approx=True) + g * jnp.exp2(s2 * h)
            part = lax.dot_general(
                shape.astype(jnp.bfloat16),
                wide,
                (((1,), (1,)), ((), ())),
                preferred_element_type=jnp.float32,
            )
            low = HALO - far
            acc[t, low : low + n, 0:COLS] = acc[t, low : low + n, 0:COLS] + part
            return 0

        lax.fori_loop(0, TP, at_point, 0, unroll=UNROLL)

    for c in range(CLASSES, 0, -1):
        def body(p, _, far=STEP * c):
            group(p, far)
            return 0

        lax.fori_loop(ends[c + 1], ends[c], body, 0)


def fold_kernel(core, inner, acc, own, other, takes):
    lane = lax.broadcasted_iota(jnp.int32, (BUCKET, LANES), 1)
    body, wing = NBUCKET * MIXES, (HALO // BUCKET) * MIXES
    half = body + wing
    begin = core * (body - wing)
    at = lax.broadcasted_iota(jnp.int32, takes.shape, 1)
    takes[...] = jnp.where((at >= begin) & (at < begin + wing * inner), 1.0, 0.0)
    for t in range(TP):
        low = acc[t, 0:BUCKET, :]
        high = jnp.zeros((BUCKET, LANES), jnp.float32)
        for i in range(1, ROWS // BUCKET):
            turned = pltpu.roll(acc[t, BUCKET * i : BUCKET * (i + 1), :], MIXES * i, 1)
            passed = lane < MIXES * i
            low = low + jnp.where(passed, 0.0, turned)
            high = high + jnp.where(passed, turned, 0.0)
        second = jnp.where(lane < LANES - half, pltpu.roll(low, LANES - half, 1), pltpu.roll(high, LANES - half, 1))
        first = jnp.where((lane < body) | (lane >= LANES - wing), pltpu.roll(low, LANES - wing, 1), 0.0)
        own[t] = jnp.where(core == 0, first, second)
        other[t] = jnp.where(core == 0, second, first)


def core_number():
    me, count = lax.axis_index("wave"), lax.axis_size("wave")
    inner = jnp.where((me > 0) & (me < count - 1), 1, 0)
    return lax.rem(me, 2), inner


def opacity(scalars, recs, tables):
    nslots = recs.shape[0]
    groups = PREP * (-(-nslots // (GROUP * PREP)))

    def kernel(scalars, recs, tables, own, other, takes, acc, *scratch):
        opacity_kernel(nslots, scalars, recs, tables, acc, *scratch)
        fold_kernel(*core_number(), acc, own, other, takes)

    return pl.pallas_call(
        kernel,
        out_shape=[jax.ShapeDtypeStruct((TP, BUCKET, LANES), jnp.float32)] * 2
        + [jax.ShapeDtypeStruct((BUCKET, NBUCKET * MIXES), jnp.float32)],
        in_specs=[SMEM, VMEM, VMEM],
        out_specs=[VMEM] * 3,
        scratch_shapes=[
            pltpu.VMEM((TP, ROWS, LANES), jnp.float32),
            pltpu.SMEM((nslots,), jnp.int32),
            pltpu.SMEM((CLASSES + 1,), jnp.int32),
            pltpu.SMEM((CLASSES + 1,), jnp.int32),
            pltpu.VMEM((GROUP * groups + 2, FIELDS, LANES), jnp.float32),
            pltpu.VMEM((groups, 5, TP, GROUP * LANES), jnp.float32),
            pltpu.VMEM((COLS, GROUP * LANES), jnp.bfloat16),
            pltpu.VMEM((ROWS, GROUP * LANES), jnp.float32),
        ],
        compiler_params=pltpu.CompilerParams(vmem_limit_bytes=24 * 2**20),
        name="opacity",
    )(scalars, recs, tables)


def per_device(
    dest_tiles,
    line_counts,
    wing_widths,
    species_ids,
    offsets,
    strengths,
    doppler,
    lorentz,
    energy,
    temp_scale,
    press_scale,
    inverse_temp,
    abundances,
):
    ntiles = lax.axis_size("wave")
    nblocks = dest_tiles.shape[1]

    def rows(array):
        return array.reshape(nblocks, LANES)

    def kernel(*refs):
        tables_kernel(*refs[9:13], refs[14])
        pack_kernel(nblocks, *refs[:9], refs[13], refs[15])

    packed, tables = pl.pallas_call(
        kernel,
        out_shape=[
            jax.ShapeDtypeStruct((2 * ntiles, FIELDS, LANES), jnp.float32),
            jax.ShapeDtypeStruct((TP * SUB + 6, FIELDS, LANES), jnp.float32),
        ],
        in_specs=[SMEM] * 3 + [VMEM] * 6 + [SMEM] * 4,
        out_specs=[VMEM] * 2,
        scratch_shapes=[pltpu.SMEM((ntiles,), jnp.int32)],
        name="pack",
    )(
        dest_tiles.reshape(nblocks),
        line_counts.reshape(nblocks),
        wing_widths.reshape(nblocks),
        rows(offsets),
        rows(doppler),
        rows(lorentz),
        rows(energy),
        rows(strengths),
        rows(species_ids),
        abundances,
        temp_scale,
        press_scale,
        inverse_temp,
    )
    cores = [list(range(core, ntiles, 2)) for core in range(2)]
    recs = lax.all_to_all(packed, "wave", split_axis=0, concat_axis=0, tiled=True, axis_index_groups=cores)
    scalars = jnp.transpose(recs[:, 6:8, 0]).astype(jnp.int32)
    own, other, takes = opacity(scalars, recs, tables)
    twin = lax.ppermute(other, "wave", [(i, i ^ 1) for i in range(ntiles)])
    shares = lax.all_to_all(own + twin, "species", split_axis=0, concat_axis=0, tiled=True)
    mine = jnp.sum(shares.reshape(-1, TP // lax.axis_size("species"), BUCKET, LANES), axis=0)

    body = NBUCKET * MIXES
    pairs = [[i, i + 1] for i in range(1, ntiles - 1, 2)] + [[0, ntiles - 1]]
    wings = lax.all_gather(mine[:, :, body:], "wave", axis_index_groups=pairs)
    middle = mine[:, :, :body] + (wings[0] + wings[1]) * takes
    middle = middle.reshape(-1, BUCKET, NBUCKET, MIXES)
    return jnp.transpose(middle, (3, 0, 2, 1)).reshape(MIXES, -1, TILE)


def solution(mesh):
    line = P("species", "wave")
    return jax.shard_map(
        per_device,
        mesh=mesh,
        in_specs=(P("species", "wave", None),) + (line,) * 8 + (P(), P(), P(), P(None, "species", None, None)),
        out_specs=P(None, "species", "wave"),
        check_vma=False,
    )
```

```python
import jax
import jax.numpy as jnp
from jax import lax
from jax.experimental import pallas as pl
from jax.experimental.pallas import tpu as pltpu
from jax.sharding import PartitionSpec as P

TILE = 256
TP = 16
MIXES = 4
SUB = 4
HALO = 64
LANES = 128
FIELDS = 8
BUCKET = 16
NBUCKET = TILE // BUCKET
ROWS = 2 * HALO + BUCKET
COLS = 2 * NBUCKET * MIXES
STEP = 8
CLASSES = HALO // STEP
UNROLL = 16
GROUP = 4
PREP = 2
POUR = 8

VMEM = pl.BlockSpec(memory_space=pltpu.VMEM)
SMEM = pl.BlockSpec(memory_space=pltpu.SMEM)


def tables_kernel(abundance, temp, press, invtemp, tables):
    at = lax.broadcasted_iota(jnp.int32, (TP, LANES), 0)
    for which, values in enumerate((temp, press, invtemp)):
        made = jnp.zeros((TP, LANES), jnp.float32)
        for t in range(TP):
            made = jnp.where(at == t, values[t], made)
        tables[TP * SUB + 2 * which] = made[:FIELDS]
        tables[TP * SUB + 2 * which + 1] = made[FIELDS:]
    mix = lax.bitwise_and(lax.broadcasted_iota(jnp.int32, (FIELDS, LANES), 0), MIXES - 1)

    def spread(t, _):
        for s in range(SUB):
            made = jnp.zeros((FIELDS, LANES), jnp.float32)
            for m in range(MIXES):
                made = jnp.where(mix == m, abundance[m, 0, s, t], made)
            tables[t * SUB + s] = made
        return 0

    lax.fori_loop(0, TP, spread, 0, unroll=16)


def pack_kernel(nblocks, dest, counts, reach, off, dop, lor, ene, stre, spec, out, used):
    ntiles = used.shape[0]
    empty = jnp.zeros((FIELDS, LANES), jnp.float32)

    def clear(tile, _):
        used[tile] = 0
        out[2 * tile] = empty
        out[2 * tile + 1] = empty
        return 0

    lax.fori_loop(0, ntiles, clear, 0, unroll=4)

    def place(block, _):
        tile = dest[block]
        rank = used[tile]
        used[tile] = rank + 1
        slot = 2 * tile + rank
        at = pl.ds(block, 1)
        out[slot, 0:1, :] = off[at, :]
        out[slot, 1:2, :] = dop[at, :]
        out[slot, 2:3, :] = lor[at, :]
        out[slot, 3:4, :] = ene[at, :]
        out[slot, 4:5, :] = stre[at, :]
        out[slot, 5:6, :] = spec[at, :].astype(jnp.float32)
        out[slot, 6:7, :] = jnp.full((1, LANES), reach[block].astype(jnp.float32))
        out[slot, 7:8, :] = jnp.full((1, LANES), counts[block].astype(jnp.float32))
        return 0

    lax.fori_loop(0, nblocks, place, 0, unroll=4)


def opacity_kernel(nslots, scalars, recs, tables, acc, order, first, lines, live, prm, hot, sq):
    def klass(i):
        wing = scalars[0, i]
        c = jnp.minimum(lax.shift_right_logical(wing, 3) + 1, CLASSES)
        return jnp.where(wing > 0, c, 0)

    share = nslots // TP

    def count(t, _):
        acc[t] = jnp.zeros(acc.shape[1:], jnp.float32)
        for j in range(share):
            i = share * t + j
            c = klass(i)
            first[c] = first[c] + 1
            lines[c] = lines[c] + scalars[1, i]
        return 0

    for c in range(CLASSES + 1):
        first[c] = 0
        lines[c] = 0
    lax.fori_loop(0, TP, count, 0, unroll=2)
    slots, total = jnp.int32(0), jnp.int32(0)
    ends = {CLASSES + 1: total}
    for c in range(CLASSES, 0, -1):
        held = first[c]
        first[c] = slots
        slots = slots + held
        total = total + lines[c]
        ends[c] = lax.div(total + (GROUP * LANES - 1), GROUP * LANES)
    first[0] = slots

    row = lax.broadcasted_iota(jnp.int32, (FIELDS, LANES), 0)
    lane = lax.broadcasted_iota(jnp.int32, (FIELDS, LANES), 1)
    blank = jnp.where((row == 1) | (row == 2), 1.0, 0.0)

    def place(i, _):
        live[i] = blank
        c = klass(i)
        at = first[c]
        order[at] = i
        first[c] = at + 1
        return 0

    lax.fori_loop(0, nslots, place, 0, unroll=8)
    for i in range(nslots, live.shape[0]):
        live[i] = blank

    def pour(i, filled):
        for j in range(POUR):
            slot = order[POUR * i + j]
            held = scalars[1, slot]
            into = lax.shift_right_logical(filled, 7)
            turn = lax.bitwise_and(filled, LANES - 1)
            side = lax.bitwise_and(lax.shift_right_logical(slot, 1), 1)
            record = jnp.where(row == 7, side.astype(jnp.float32), recs[slot])
            turned = pltpu.roll(record, turn, 1)
            pltpu.store(live.at[into], turned, mask=(lane >= turn) & (lane < turn + held))
            pltpu.store(live.at[into + 1], turned, mask=lane < turn + held - LANES)
            filled = filled + held
        return filled

    lax.fori_loop(0, lax.div(slots + (POUR - 1), POUR), pour, jnp.int32(0))

    def column(which):
        made = jnp.concatenate([tables[TP * SUB + 2 * which], tables[TP * SUB + 2 * which + 1]], axis=0)
        return jnp.concatenate([made] * GROUP, axis=1)

    tscale, pscale, invt = column(0), column(1), column(2)
    bucket_row = lax.shift_right_logical(lax.broadcasted_iota(jnp.int32, (COLS, GROUP * LANES), 0), 2)
    bucket_row = bucket_row.astype(jnp.float32)

    def prepare(p):
        rec = jnp.concatenate([live[GROUP * p + j] for j in range(GROUP)], axis=1)
        dop, lor, energy = rec[1:2], rec[2:3], rec[3:4]
        gauss = 2.35482 * (tscale * dop)
        lorz = 2.0 * (pscale * lor)
        g2, l2 = gauss * gauss, lorz * lorz
        g4, l4 = g2 * g2, l2 * l2
        fifth = (
            g4 * gauss
            + 2.69269 * g4 * lorz
            + 2.42843 * (g2 * gauss) * l2
            + 4.47163 * g2 * (l2 * lorz)
            + 0.07842 * gauss * l4
            + l4 * lorz
        )
        width = jnp.exp(0.2 * jnp.log(fifth))
        inv = 1.0 / width
        q = lorz * inv
        mixing = q * (1.36603 + q * (-0.47719 + q * 0.11116))
        prm[p, 0] = mixing * (0.15915494 * width)
        prm[p, 1] = 0.25 * (width * width)
        prm[p, 2] = (1.0 - mixing) * (0.9394373 * inv)
        prm[p, 3] = (-2.7725887 * 1.4426950408889634) * (inv * inv)
        prm[p, 4] = rec[4:5] * jnp.exp(-(invt * energy))

    def prepare_some(i, _):
        for j in range(PREP):
            prepare(PREP * i + j)
        return 0

    lax.fori_loop(0, lax.div(ends[1] + (PREP - 1), PREP), prepare_some, 0)

    def group(p, far):
        n = 2 * far + BUCKET
        rec = jnp.concatenate([live[GROUP * p + j] for j in range(GROUP)], axis=1)
        center, kind, limit, side = rec[0:1], rec[5:6], rec[6:7], rec[7:8]
        bucket = jnp.minimum(jnp.floor(center * (1.0 / BUCKET)), NBUCKET - 1.0)
        frac = center - BUCKET * bucket
        hot[...] = jnp.where(bucket_row == bucket + NBUCKET * side, 1.0, 0.0).astype(jnp.bfloat16)
        point = lax.broadcasted_iota(jnp.int32, (n, GROUP * LANES), 0).astype(jnp.float32) - float(far)
        x = point - frac
        sq[0:n] = jnp.where(jnp.abs(x) <= limit, x * x, jnp.inf)

        def at_point(t, _):
            at = pl.ds(t, 1)
            picked = jnp.concatenate([tables[t * SUB]] * GROUP, axis=1)
            for s in range(1, SUB):
                ab = tables[t * SUB + s]
                picked = jnp.where(kind == float(s), jnp.concatenate([ab] * GROUP, axis=1), picked)
            w8 = picked * prm[p, 4, at, :]
            w16 = jnp.concatenate([w8, w8], axis=0).astype(jnp.bfloat16)
            wide = hot[...] * jnp.concatenate([w16] * (COLS // 16), axis=0)
            a, b, g, h = [prm[p, j, at, :] for j in range(4)]
            s2 = sq[0:n]
            shape = a * pl.reciprocal(s2 + b, approx=True) + g * jnp.exp2(s2 * h)
            part = lax.dot_general(
                shape.astype(jnp.bfloat16),
                wide,
                (((1,), (1,)), ((), ())),
                preferred_element_type=jnp.float32,
            )
            low = HALO - far
            acc[t, low : low + n, 0:COLS] = acc[t, low : low + n, 0:COLS] + part
            return 0

        lax.fori_loop(0, TP, at_point, 0, unroll=UNROLL)

    for c in range(CLASSES, 0, -1):
        def body(p, _, far=STEP * c):
            group(p, far)
            return 0

        lax.fori_loop(ends[c + 1], ends[c], body, 0)


def fold_kernel(core, inner, acc, own, other, takes):
    lane = lax.broadcasted_iota(jnp.int32, (BUCKET, LANES), 1)
    body, wing = NBUCKET * MIXES, (HALO // BUCKET) * MIXES
    half = body + wing
    begin = core * (body - wing)
    at = lax.broadcasted_iota(jnp.int32, takes.shape, 1)
    takes[...] = jnp.where((at >= begin) & (at < begin + wing * inner), 1.0, 0.0)
    for t in range(TP):
        low = acc[t, 0:BUCKET, :]
        high = jnp.zeros((BUCKET, LANES), jnp.float32)
        for i in range(1, ROWS // BUCKET):
            turned = pltpu.roll(acc[t, BUCKET * i : BUCKET * (i + 1), :], MIXES * i, 1)
            passed = lane < MIXES * i
            low = low + jnp.where(passed, 0.0, turned)
            high = high + jnp.where(passed, turned, 0.0)
        second = jnp.where(lane < LANES - half, pltpu.roll(low, LANES - half, 1), pltpu.roll(high, LANES - half, 1))
        first = jnp.where((lane < body) | (lane >= LANES - wing), pltpu.roll(low, LANES - wing, 1), 0.0)
        own[t] = jnp.where(core == 0, first, second)
        other[t] = jnp.where(core == 0, second, first)


def core_number():
    me, count = lax.axis_index("wave"), lax.axis_size("wave")
    inner = jnp.where((me > 0) & (me < count - 1), 1, 0)
    return lax.rem(me, 2), inner


def opacity(scalars, recs, tables):
    nslots = recs.shape[0]
    groups = PREP * (-(-nslots // (GROUP * PREP)))

    def kernel(scalars, recs, tables, own, other, takes, acc, *scratch):
        opacity_kernel(nslots, scalars, recs, tables, acc, *scratch)
        fold_kernel(*core_number(), acc, own, other, takes)

    return pl.pallas_call(
        kernel,
        out_shape=[jax.ShapeDtypeStruct((TP, BUCKET, LANES), jnp.float32)] * 2
        + [jax.ShapeDtypeStruct((BUCKET, NBUCKET * MIXES), jnp.float32)],
        in_specs=[SMEM, VMEM, VMEM],
        out_specs=[VMEM] * 3,
        scratch_shapes=[
            pltpu.VMEM((TP, ROWS, LANES), jnp.float32),
            pltpu.SMEM((nslots,), jnp.int32),
            pltpu.SMEM((CLASSES + 1,), jnp.int32),
            pltpu.SMEM((CLASSES + 1,), jnp.int32),
            pltpu.VMEM((GROUP * groups + 2, FIELDS, LANES), jnp.float32),
            pltpu.VMEM((groups, 5, TP, GROUP * LANES), jnp.float32),
            pltpu.VMEM((COLS, GROUP * LANES), jnp.bfloat16),
            pltpu.VMEM((ROWS, GROUP * LANES), jnp.float32),
        ],
        compiler_params=pltpu.CompilerParams(vmem_limit_bytes=24 * 2**20),
        name="opacity",
    )(scalars, recs, tables)


def per_device(
    dest_tiles,
    line_counts,
    wing_widths,
    species_ids,
    offsets,
    strengths,
    doppler,
    lorentz,
    energy,
    temp_scale,
    press_scale,
    inverse_temp,
    abundances,
):
    ntiles = lax.axis_size("wave")
    nblocks = dest_tiles.shape[1]

    def rows(array):
        return array.reshape(nblocks, LANES)

    def kernel(*refs):
        tables_kernel(*refs[9:13], refs[14])
        pack_kernel(nblocks, *refs[:9], refs[13], refs[15])

    packed, tables = pl.pallas_call(
        kernel,
        out_shape=[
            jax.ShapeDtypeStruct((2 * ntiles, FIELDS, LANES), jnp.float32),
            jax.ShapeDtypeStruct((TP * SUB + 6, FIELDS, LANES), jnp.float32),
        ],
        in_specs=[SMEM] * 3 + [VMEM] * 6 + [SMEM] * 4,
        out_specs=[VMEM] * 2,
        scratch_shapes=[pltpu.SMEM((ntiles,), jnp.int32)],
        name="pack",
    )(
        dest_tiles.reshape(nblocks),
        line_counts.reshape(nblocks),
        wing_widths.reshape(nblocks),
        rows(offsets),
        rows(doppler),
        rows(lorentz),
        rows(energy),
        rows(strengths),
        rows(species_ids),
        abundances,
        temp_scale,
        press_scale,
        inverse_temp,
    )
    cores = [list(range(core, ntiles, 2)) for core in range(2)]
    recs = lax.all_to_all(packed, "wave", split_axis=0, concat_axis=0, tiled=True, axis_index_groups=cores)
    scalars = jnp.transpose(recs[:, 6:8, 0]).astype(jnp.int32)
    own, other, takes = opacity(scalars, recs, tables)
    twin = lax.ppermute(other, "wave", [(i, i ^ 1) for i in range(ntiles)])
    shares = lax.all_to_all(own + twin, "species", split_axis=0, concat_axis=0, tiled=True)
    mine = jnp.sum(shares.reshape(-1, TP // lax.axis_size("species"), BUCKET, LANES), axis=0)

    body = NBUCKET * MIXES
    pairs = [[i, i + 1] for i in range(1, ntiles - 1, 2)] + [[0, ntiles - 1]]
    wings = lax.all_gather(mine[:, :, body:], "wave", axis_index_groups=pairs)
    middle = mine[:, :, :body] + (wings[0] + wings[1]) * takes
    middle = middle.reshape(-1, BUCKET, NBUCKET, MIXES)
    return jnp.transpose(middle, (3, 0, 2, 1)).reshape(MIXES, -1, TILE)


def solution(mesh):
    line = P("species", "wave")
    return jax.shard_map(
        per_device,
        mesh=mesh,
        in_specs=(P("species", "wave", None),) + (line,) * 8 + (P(), P(), P(), P(None, "species", None, None)),
        out_specs=P(None, "species", "wave"),
        check_vma=False,
    )
```

```python
import jax
import jax.numpy as jnp
from jax import lax
from jax.experimental import pallas as pl
from jax.experimental.pallas import tpu as pltpu
from jax.sharding import PartitionSpec as P

TILE = 256
TP = 16
MIXES = 4
SUB = 4
HALO = 64
LANES = 128
FIELDS = 8
BUCKET = 16
NBUCKET = TILE // BUCKET
ROWS = 2 * HALO + BUCKET
COLS = 2 * NBUCKET * MIXES
STEP = 8
CLASSES = HALO // STEP
UNROLL = 16
GROUP = 4
PREP = 2
POUR = 8

VMEM = pl.BlockSpec(memory_space=pltpu.VMEM)
SMEM = pl.BlockSpec(memory_space=pltpu.SMEM)


def tables_kernel(abundance, temp, press, invtemp, tables):
    at = lax.broadcasted_iota(jnp.int32, (TP, LANES), 0)
    for which, values in enumerate((temp, press, invtemp)):
        made = jnp.zeros((TP, LANES), jnp.float32)
        for t in range(TP):
            made = jnp.where(at == t, values[t], made)
        tables[TP * SUB + 2 * which] = made[:FIELDS]
        tables[TP * SUB + 2 * which + 1] = made[FIELDS:]
    mix = lax.bitwise_and(lax.broadcasted_iota(jnp.int32, (FIELDS, LANES), 0), MIXES - 1)

    def spread(t, _):
        for s in range(SUB):
            made = jnp.zeros((FIELDS, LANES), jnp.float32)
            for m in range(MIXES):
                made = jnp.where(mix == m, abundance[m, 0, s, t], made)
            tables[t * SUB + s] = made
        return 0

    lax.fori_loop(0, TP, spread, 0, unroll=16)


def pack_kernel(nblocks, dest, counts, reach, off, dop, lor, ene, stre, spec, out, used):
    ntiles = used.shape[0]
    empty = jnp.zeros((FIELDS, LANES), jnp.float32)

    def clear(tile, _):
        used[tile] = 0
        out[2 * tile] = empty
        out[2 * tile + 1] = empty
        return 0

    lax.fori_loop(0, ntiles, clear, 0, unroll=4)

    def place(block, _):
        tile = dest[block]
        rank = used[tile]
        used[tile] = rank + 1
        slot = 2 * tile + rank
        at = pl.ds(block, 1)
        out[slot, 0:1, :] = off[at, :]
        out[slot, 1:2, :] = dop[at, :]
        out[slot, 2:3, :] = lor[at, :]
        out[slot, 3:4, :] = ene[at, :]
        out[slot, 4:5, :] = stre[at, :]
        out[slot, 5:6, :] = spec[at, :].astype(jnp.float32)
        out[slot, 6:7, :] = jnp.full((1, LANES), reach[block].astype(jnp.float32))
        out[slot, 7:8, :] = jnp.full((1, LANES), counts[block].astype(jnp.float32))
        return 0

    lax.fori_loop(0, nblocks, place, 0, unroll=8)


def opacity_kernel(nslots, scalars, recs, tables, acc, order, first, lines, live, prm, hot, sq):
    def klass(i):
        wing = scalars[0, i]
        c = jnp.minimum(lax.shift_right_logical(wing, 3) + 1, CLASSES)
        return jnp.where(wing > 0, c, 0)

    share = nslots // TP

    def count(t, _):
        acc[t] = jnp.zeros(acc.shape[1:], jnp.float32)
        for j in range(share):
            i = share * t + j
            c = klass(i)
            first[c] = first[c] + 1
            lines[c] = lines[c] + scalars[1, i]
        return 0

    for c in range(CLASSES + 1):
        first[c] = 0
        lines[c] = 0
    lax.fori_loop(0, TP, count, 0, unroll=2)
    slots, total = jnp.int32(0), jnp.int32(0)
    ends = {CLASSES + 1: total}
    for c in range(CLASSES, 0, -1):
        held = first[c]
        first[c] = slots
        slots = slots + held
        total = total + lines[c]
        ends[c] = lax.div(total + (GROUP * LANES - 1), GROUP * LANES)
    first[0] = slots

    row = lax.broadcasted_iota(jnp.int32, (FIELDS, LANES), 0)
    lane = lax.broadcasted_iota(jnp.int32, (FIELDS, LANES), 1)
    blank = jnp.where((row == 1) | (row == 2), 1.0, 0.0)

    def place(i, _):
        live[i] = blank
        c = klass(i)
        at = first[c]
        order[at] = i
        first[c] = at + 1
        return 0

    lax.fori_loop(0, nslots, place, 0, unroll=8)
    for i in range(nslots, live.shape[0]):
        live[i] = blank

    def pour(i, filled):
        for j in range(POUR):
            slot = order[POUR * i + j]
            held = scalars[1, slot]
            into = lax.shift_right_logical(filled, 7)
            turn = lax.bitwise_and(filled, LANES - 1)
            side = lax.bitwise_and(lax.shift_right_logical(slot, 1), 1)
            record = jnp.where(row == 7, side.astype(jnp.float32), recs[slot])
            turned = pltpu.roll(record, turn, 1)
            pltpu.store(live.at[into], turned, mask=(lane >= turn) & (lane < turn + held))
            pltpu.store(live.at[into + 1], turned, mask=lane < turn + held - LANES)
            filled = filled + held
        return filled

    lax.fori_loop(0, lax.div(slots + (POUR - 1), POUR), pour, jnp.int32(0))

    def column(which):
        made = jnp.concatenate([tables[TP * SUB + 2 * which], tables[TP * SUB + 2 * which + 1]], axis=0)
        return jnp.concatenate([made] * GROUP, axis=1)

    tscale, pscale, invt = column(0), column(1), column(2)
    bucket_row = lax.shift_right_logical(lax.broadcasted_iota(jnp.int32, (COLS, GROUP * LANES), 0), 2)
    bucket_row = bucket_row.astype(jnp.float32)

    def prepare(p):
        rec = jnp.concatenate([live[GROUP * p + j] for j in range(GROUP)], axis=1)
        dop, lor, energy = rec[1:2], rec[2:3], rec[3:4]
        gauss = 2.35482 * (tscale * dop)
        lorz = 2.0 * (pscale * lor)
        g2, l2 = gauss * gauss, lorz * lorz
        g4, l4 = g2 * g2, l2 * l2
        fifth = (
            g4 * gauss
            + 2.69269 * g4 * lorz
            + 2.42843 * (g2 * gauss) * l2
            + 4.47163 * g2 * (l2 * lorz)
            + 0.07842 * gauss * l4
            + l4 * lorz
        )
        width = jnp.exp(0.2 * jnp.log(fifth))
        inv = pl.reciprocal(width, approx=True)
        q = lorz * inv
        mixing = q * (1.36603 + q * (-0.47719 + q * 0.11116))
        prm[p, 0] = mixing * (0.15915494 * width)
        prm[p, 1] = 0.25 * (width * width)
        prm[p, 2] = (1.0 - mixing) * (0.9394373 * inv)
        prm[p, 3] = (-2.7725887 * 1.4426950408889634) * (inv * inv)
        prm[p, 4] = rec[4:5] * jnp.exp(-(invt * energy))

    def prepare_some(i, _):
        for j in range(PREP):
            prepare(PREP * i + j)
        return 0

    lax.fori_loop(0, lax.div(ends[1] + (PREP - 1), PREP), prepare_some, 0)

    def group(p, far):
        n = 2 * far + BUCKET
        rec = jnp.concatenate([live[GROUP * p + j] for j in range(GROUP)], axis=1)
        center, kind, limit, side = rec[0:1], rec[5:6], rec[6:7], rec[7:8]
        bucket = jnp.minimum(jnp.floor(center * (1.0 / BUCKET)), NBUCKET - 1.0)
        frac = center - BUCKET * bucket
        hot[...] = jnp.where(bucket_row == bucket + NBUCKET * side, 1.0, 0.0).astype(jnp.bfloat16)
        point = lax.broadcasted_iota(jnp.int32, (n, GROUP * LANES), 0).astype(jnp.float32) - float(far)
        x = point - frac
        sq[0:n] = jnp.where(jnp.abs(x) <= limit, x * x, jnp.inf)

        def at_point(t, _):
            at = pl.ds(t, 1)
            picked = jnp.concatenate([tables[t * SUB]] * GROUP, axis=1)
            for s in range(1, SUB):
                ab = tables[t * SUB + s]
                picked = jnp.where(kind == float(s), jnp.concatenate([ab] * GROUP, axis=1), picked)
            w8 = picked * prm[p, 4, at, :]
            w16 = jnp.concatenate([w8, w8], axis=0).astype(jnp.bfloat16)
            wide = hot[...] * jnp.concatenate([w16] * (COLS // 16), axis=0)
            a, b, g, h = [prm[p, j, at, :] for j in range(4)]
            s2 = sq[0:n]
            shape = a * pl.reciprocal(s2 + b, approx=True) + g * jnp.exp2(s2 * h)
            part = lax.dot_general(
                shape.astype(jnp.bfloat16),
                wide,
                (((1,), (1,)), ((), ())),
                preferred_element_type=jnp.float32,
            )
            low = HALO - far
            acc[t, low : low + n, 0:COLS] = acc[t, low : low + n, 0:COLS] + part
            return 0

        lax.fori_loop(0, TP, at_point, 0, unroll=UNROLL)

    for c in range(CLASSES, 0, -1):
        def body(p, _, far=STEP * c):
            group(p, far)
            return 0

        lax.fori_loop(ends[c + 1], ends[c], body, 0)


def fold_kernel(core, inner, acc, own, other, takes):
    lane = lax.broadcasted_iota(jnp.int32, (BUCKET, LANES), 1)
    body, wing = NBUCKET * MIXES, (HALO // BUCKET) * MIXES
    half = body + wing
    begin = core * (body - wing)
    at = lax.broadcasted_iota(jnp.int32, takes.shape, 1)
    takes[...] = jnp.where((at >= begin) & (at < begin + wing * inner), 1.0, 0.0)
    for t in range(TP):
        low = acc[t, 0:BUCKET, :]
        high = jnp.zeros((BUCKET, LANES), jnp.float32)
        for i in range(1, ROWS // BUCKET):
            turned = pltpu.roll(acc[t, BUCKET * i : BUCKET * (i + 1), :], MIXES * i, 1)
            passed = lane < MIXES * i
            low = low + jnp.where(passed, 0.0, turned)
            high = high + jnp.where(passed, turned, 0.0)
        second = jnp.where(lane < LANES - half, pltpu.roll(low, LANES - half, 1), pltpu.roll(high, LANES - half, 1))
        first = jnp.where((lane < body) | (lane >= LANES - wing), pltpu.roll(low, LANES - wing, 1), 0.0)
        own[t] = jnp.where(core == 0, first, second)
        other[t] = jnp.where(core == 0, second, first)


def core_number():
    me, count = lax.axis_index("wave"), lax.axis_size("wave")
    inner = jnp.where((me > 0) & (me < count - 1), 1, 0)
    return lax.rem(me, 2), inner


def opacity(scalars, recs, tables):
    nslots = recs.shape[0]
    groups = PREP * (-(-nslots // (GROUP * PREP)))

    def kernel(scalars, recs, tables, own, other, takes, acc, *scratch):
        opacity_kernel(nslots, scalars, recs, tables, acc, *scratch)
        fold_kernel(*core_number(), acc, own, other, takes)

    return pl.pallas_call(
        kernel,
        out_shape=[jax.ShapeDtypeStruct((TP, BUCKET, LANES), jnp.float32)] * 2
        + [jax.ShapeDtypeStruct((BUCKET, NBUCKET * MIXES), jnp.float32)],
        in_specs=[SMEM, VMEM, VMEM],
        out_specs=[VMEM] * 3,
        scratch_shapes=[
            pltpu.VMEM((TP, ROWS, LANES), jnp.float32),
            pltpu.SMEM((nslots,), jnp.int32),
            pltpu.SMEM((CLASSES + 1,), jnp.int32),
            pltpu.SMEM((CLASSES + 1,), jnp.int32),
            pltpu.VMEM((GROUP * groups + 2, FIELDS, LANES), jnp.float32),
            pltpu.VMEM((groups, 5, TP, GROUP * LANES), jnp.float32),
            pltpu.VMEM((COLS, GROUP * LANES), jnp.bfloat16),
            pltpu.VMEM((ROWS, GROUP * LANES), jnp.float32),
        ],
        compiler_params=pltpu.CompilerParams(vmem_limit_bytes=24 * 2**20),
        name="opacity",
    )(scalars, recs, tables)


def per_device(
    dest_tiles,
    line_counts,
    wing_widths,
    species_ids,
    offsets,
    strengths,
    doppler,
    lorentz,
    energy,
    temp_scale,
    press_scale,
    inverse_temp,
    abundances,
):
    ntiles = lax.axis_size("wave")
    nblocks = dest_tiles.shape[1]

    def rows(array):
        return array.reshape(nblocks, LANES)

    def kernel(*refs):
        tables_kernel(*refs[9:13], refs[14])
        pack_kernel(nblocks, *refs[:9], refs[13], refs[15])

    packed, tables = pl.pallas_call(
        kernel,
        out_shape=[
            jax.ShapeDtypeStruct((2 * ntiles, FIELDS, LANES), jnp.float32),
            jax.ShapeDtypeStruct((TP * SUB + 6, FIELDS, LANES), jnp.float32),
        ],
        in_specs=[SMEM] * 3 + [VMEM] * 6 + [SMEM] * 4,
        out_specs=[VMEM] * 2,
        scratch_shapes=[pltpu.SMEM((ntiles,), jnp.int32)],
        name="pack",
    )(
        dest_tiles.reshape(nblocks),
        line_counts.reshape(nblocks),
        wing_widths.reshape(nblocks),
        rows(offsets),
        rows(doppler),
        rows(lorentz),
        rows(energy),
        rows(strengths),
        rows(species_ids),
        abundances,
        temp_scale,
        press_scale,
        inverse_temp,
    )
    cores = [list(range(core, ntiles, 2)) for core in range(2)]
    recs = lax.all_to_all(packed, "wave", split_axis=0, concat_axis=0, tiled=True, axis_index_groups=cores)
    scalars = jnp.transpose(recs[:, 6:8, 0]).astype(jnp.int32)
    own, other, takes = opacity(scalars, recs, tables)
    twin = lax.ppermute(other, "wave", [(i, i ^ 1) for i in range(ntiles)])
    shares = lax.all_to_all(own + twin, "species", split_axis=0, concat_axis=0, tiled=True)
    mine = jnp.sum(shares.reshape(-1, TP // lax.axis_size("species"), BUCKET, LANES), axis=0)

    body = NBUCKET * MIXES
    pairs = [[i, i + 1] for i in range(1, ntiles - 1, 2)] + [[0, ntiles - 1]]
    wings = lax.all_gather(mine[:, :, body:], "wave", axis_index_groups=pairs)
    middle = mine[:, :, :body] + (wings[0] + wings[1]) * takes
    middle = middle.reshape(-1, BUCKET, NBUCKET, MIXES)
    return jnp.transpose(middle, (3, 0, 2, 1)).reshape(MIXES, -1, TILE)


def solution(mesh):
    line = P("species", "wave")
    return jax.shard_map(
        per_device,
        mesh=mesh,
        in_specs=(P("species", "wave", None),) + (line,) * 8 + (P(), P(), P(), P(None, "species", None, None)),
        out_specs=P(None, "species", "wave"),
        check_vma=False,
    )
```
